128 devices in a mesh: gx: 8 (over z_lo, y), gy: 16 (over z_hi, x, core).
Axes of the slice: x: 4, y: 4, z: 4 (z_hi: 2, z_lo: 2; z = z_hi * 2 + z_lo), core: 2. Of those that a mesh axis runs over, the one named last changes fastest.
Arguments:
- adjoint_prev: float32 [2, 20, 512, 2048], P(None, None, 'gx', 'gy'), may hold values from -2 to 2
- viscosity: float32 [20, 512, 2048], P(None, 'gx', 'gy'), may hold values from 0.5 to 4
- friction: float32 [512, 2048], P('gx', 'gy'), may hold values from 0.5 to 20
- basal_velocity: float32 [2, 512, 2048], P(None, 'gx', 'gy'), may hold values from -6 to 6
- ice_mask: int32 [512, 2048], P('gx', 'gy'), may hold values 0 or 1
- misfit: bfloat16 [131072, 2, 128], P(('gx', 'gy')), may hold values from -60 to 60
- block_tile: int32 [131072, 1], P(('gx', 'gy')), may hold values from 0 to 127; in each aligned block of 1024 rows (0 to 1023, 1024 to 2047, ...) at most 16 rows name the same one
- block_row: int32 [131072], P(('gx', 'gy')), may hold values from 0 to 63
Outputs:
- adjoint: float32 [2, 20, 512, 2048], P(None, None, 'gx', 'gy')
- gradient: float32 [512, 2048], P('gx', 'gy')
The draws below stay inside these ranges and needn't reach their ends.
Inputs may be any that keep to these rules, and one draw needn't show every extreme that they name: `block_tile`: among the 1024 blocks of one device no tile is named more than 16 times, a bound that some block reaches.
All inputs are finite; a program needn't handle non-finite values. No bound on the sum of `ice_mask` on one device may be relied on, other than what follows from the above.
Results may differ from the reference program's by a relative error of at most 0.0003.
Values may be sent and summed in bfloat16 or wider, within the bound.
A program may use at most 64 MiB of HBM per device.

```python
import math
import jax
import jax.numpy as jnp
import numpy as np

TX = 64
TY = 128
LAYERS = 20
ITERS = 3
SB = 1024
CAP = 16
NX = 512
NY = 2048
BLOCKS = 131072
N_GY = 16
DEVICES = 128


def with_ends(result, own_key, least, largest):
    extent = result.shape
    place = [jax.random.randint(jax.random.fold_in(own_key, axis), (), 0, extent[axis]) for axis in range(len(extent))]
    result = result.at[tuple(place)].set(least)
    longest = extent.index(max(extent))
    place[longest] = (place[longest] + 1) % extent[longest]
    return result.at[tuple(place)].set(largest)


def block_levels(rng, extent, shards, least, largest):
    loudness = 1.0
    for axis_at, shards_of in shards:
        draws = jax.random.uniform(jax.random.fold_in(jax.random.fold_in(rng, 6), axis_at), (shards_of,), jnp.float32, least / len(shards), largest / len(shards))
        loudness = loudness * jnp.repeat(jnp.exp(draws), extent[axis_at] // shards_of).reshape((-1,) + (1,) * (len(extent) - 1 - axis_at))
    return loudness


def routed_block(key, own, number, rows, amount, top, bound, skew):
    sequence = jax.random.permutation(key, amount)
    heavy_load, usual = load_shares(amount, rows * top, bound, skew, True), load_shares(amount, rows * top, bound, skew, False)
    places = jnp.arange(amount)

    def named(tallies, turn):
        used = int((tallies > 0).sum())
        fixed = max(1, used // 4)
        shifted = fixed + (places - fixed + turn * (used - fixed)) % max(1, amount - fixed)
        return jnp.zeros((amount,), jnp.int32).at[sequence[jnp.where(places < fixed, places, shifted)]].set(jnp.asarray(tallies, jnp.int32))

    tallies = jnp.where(number % 4 == 0, named(heavy_load, number // 4), named(usual, number - number // 4 - 1))
    mixed = jax.random.permutation(jax.random.fold_in(own, 3), amount)
    giver, sink = mixed[0:amount // 2 * 2:2], mixed[1:amount // 2 * 2:2]
    margin = jnp.minimum(tallies[giver] - 1, bound - tallies[sink]) // 2
    margin = jnp.where((giver == sequence[0]) | (sink == sequence[0]) | (tallies[sink] == 0), 0, jnp.maximum(margin, 0))
    shifted = jax.random.randint(jax.random.fold_in(own, 4), (amount // 2,), 0, 1 << 20) % (margin + 1)
    tallies = tallies.at[giver].add(-shifted).at[sink].add(shifted)
    labels = jnp.searchsorted(jnp.cumsum(tallies), jnp.arange(rows * top), side="right").astype(jnp.int32)
    listing = labels.reshape(top, rows).T
    listing = listing[jax.random.permutation(jax.random.fold_in(own, 1), rows)]
    turn = jax.random.randint(jax.random.fold_in(own, 2), (rows, 1), 0, top)
    return jnp.take_along_axis(listing, (jnp.arange(top)[None, :] + turn) % top, axis=1)


def load_shares(count, total, limit, lean, full):
    loads = [(1 << 20) // math.isqrt(grade ** lean) + 1 for grade in range(1, count + 1)]
    largest = limit if full else min(limit, max(-(-total // count), total * loads[0] // sum(loads)))
    least = 1 if total - largest >= count - 1 else 0
    counts, rest = [largest] + [least] * (count - 1), total - largest - least * (count - 1)
    while rest > 0:
        movable = [i for i in range(1, count) if counts[i] < largest] or [i for i in range(1, count) if counts[i] < limit]
        mass, budget = sum([loads[i] for i in movable]), rest
        for i in movable:
            more = min(limit - counts[i], max(1, budget * loads[i] // mass), rest)
            counts[i] = counts[i] + more
            rest = rest - more
    return np.array(counts)


def gaussian(key, shape, spread, bound, split=(), kind=jnp.bfloat16):
    entries = spread * jax.random.normal(key, shape, jnp.float32)
    if split:
        entries = entries * block_levels(key, shape, split, -0.22, 0.18)
    return jnp.clip(entries, -bound, bound).astype(kind)


def setup_inputs(seed: int = 0) -> dict:
    seeds = jax.random.split(jax.random.key(seed), 9)
    adjoint_prev = gaussian(seeds[0], (2, LAYERS, NX, NY), 0.3, 2.0, ((2, 8), (3, 16)), jnp.float32)
    viscosity = jnp.clip(jnp.exp(math.log(4.0) - 2.0794415 * jax.random.uniform(seeds[1], (LAYERS, NX, NY), jnp.float32) ** block_levels(seeds[1], (LAYERS, NX, NY), ((1, 8), (2, 16)), -0.2, 0.2)), 0.5, 4.0)
    friction = jnp.clip(jnp.exp(math.log(20.0) - 3.6888795 * jax.random.uniform(seeds[2], (NX, NY), jnp.float32) ** block_levels(seeds[2], (NX, NY), ((0, 8), (1, 16)), -0.2, 0.2)), 0.5, 20.0)
    basal_velocity = gaussian(seeds[3], (2, NX, NY), 1.0, 6.0, ((1, 8), (2, 16)), jnp.float32)
    ice_mask = with_ends((jax.random.randint(seeds[4], (NX, NY), 0, 4) < 3).astype(jnp.int32), jax.random.fold_in(seeds[4], 1), 0, 1)
    misfit = gaussian(seeds[5], (BLOCKS, 2, TY), 10.0, 60.0, ((0, 128),))
    block_tile_keys = jax.random.split(jax.random.fold_in(seeds[6], 1), BLOCKS // SB)
    block_tile_turns = jax.random.permutation(jax.random.fold_in(seeds[6], 3), BLOCKS // SB)
    block_tile = jax.vmap(lambda own, number: routed_block(jax.random.fold_in(seeds[6], 2), own, number, SB, DEVICES, 1, CAP, 2))(block_tile_keys, block_tile_turns).reshape((BLOCKS, 1))
    block_row = with_ends(jax.random.randint(seeds[7], (BLOCKS,), 0, TX), jax.random.fold_in(seeds[7], 1), 0, TX - 1).astype(jnp.int32)
    return dict(adjoint_prev=adjoint_prev, viscosity=viscosity, friction=friction, basal_velocity=basal_velocity, ice_mask=ice_mask, misfit=misfit, block_tile=block_tile, block_row=block_row)


VERTICAL = 4.0


def omega_list(count):
    return [1.0 / (1.3 + 1.2 * math.cos((2 * turn_id + 1) * math.pi / (2 * count))) for turn_id in range(count)]


def padded_of(values):
    widths = [(0, 0)] * (values.ndim - 2) + [(1, 1), (1, 1)]
    return jnp.pad(values, widths)


def coefficients(padded_eta, friction):
    center = padded_eta[:, 1:-1, 1:-1]
    x_low = 0.5 * (padded_eta[:, :-2, 1:-1] + center)
    x_high = 0.5 * (padded_eta[:, 2:, 1:-1] + center)
    y_low = 0.5 * (padded_eta[:, 1:-1, :-2] + center)
    y_high = 0.5 * (padded_eta[:, 1:-1, 2:] + center)
    layer_face = 0.5 * (center[:-1] + center[1:])
    zero_face = jnp.zeros_like(center[:1])
    z_up = jnp.concatenate([zero_face, layer_face], axis=0)
    z_down = jnp.concatenate([layer_face, zero_face], axis=0)
    basal = jnp.concatenate([jnp.zeros_like(center[:-1]), friction[None].astype(jnp.float32)], axis=0)
    horiz_x = x_low + x_high
    horiz_y = y_low + y_high
    vertical = VERTICAL * (z_up + z_down) + basal
    diagonal = jnp.stack([4.0 * horiz_x + horiz_y + vertical, horiz_x + 4.0 * horiz_y + vertical])
    return (x_low, x_high, y_low, y_high, z_up, z_down, basal), diagonal


def diffuse(padded, coeff, weight_x, weight_y):
    x_low, x_high, y_low, y_high, z_up, z_down, basal = coeff
    center = padded[:, 1:-1, 1:-1]
    zero_layer = jnp.zeros_like(center[:1])
    above = jnp.concatenate([zero_layer, center[:-1]], axis=0)
    below = jnp.concatenate([center[1:], zero_layer], axis=0)
    total = weight_x * (x_low * (center - padded[:, :-2, 1:-1]) + x_high * (center - padded[:, 2:, 1:-1]))
    total = total + weight_y * (y_low * (center - padded[:, 1:-1, :-2]) + y_high * (center - padded[:, 1:-1, 2:]))
    total = total + VERTICAL * (z_up * (center - above) + z_down * (center - below))
    return total + basal * center


def mixed(padded, padded_eta, weight_x, weight_y):
    along_y = 0.5 * (padded[:, :, 2:] - padded[:, :, :-2])
    flux_x = weight_x * padded_eta[:, :, 1:-1] * along_y
    along_x = 0.5 * (padded[:, 2:, :] - padded[:, :-2, :])
    flux_y = weight_y * padded_eta[:, 1:-1, :] * along_x
    return -(0.5 * (flux_x[:, 2:] - flux_x[:, :-2]) + 0.5 * (flux_y[:, :, 2:] - flux_y[:, :, :-2]))


def operate(padded_adj, padded_eta, coeff):
    first = diffuse(padded_adj[0], coeff, 4.0, 1.0) + mixed(padded_adj[1], padded_eta, 2.0, 1.0)
    second = diffuse(padded_adj[1], coeff, 1.0, 4.0) + mixed(padded_adj[0], padded_eta, 1.0, 2.0)
    return jnp.stack([first, second])


def reference(adjoint_prev, viscosity, friction, basal_velocity, ice_mask, misfit, block_tile, block_row):
    padded_eta = padded_of(viscosity)
    coeff, diagonal = coefficients(padded_eta, friction)
    ice = ice_mask.astype(jnp.float32)
    target = block_tile[:, 0].astype(jnp.int32)
    tile_x = target // N_GY
    tile_y = target % N_GY
    global_row = (tile_x * TX + block_row).astype(jnp.int32)
    values = jnp.transpose(misfit.astype(jnp.float32), (1, 0, 2))
    surface = jnp.zeros((2, NX, N_GY, TY), jnp.float32).at[:, global_row, tile_y, :].add(values)
    source = jnp.zeros((2, LAYERS, NX, NY), jnp.float32).at[:, 0].set(surface.reshape(2, NX, NY))
    adjoint = ice * adjoint_prev
    for omega in omega_list(ITERS):
        image = operate(padded_of(adjoint), padded_eta, coeff)
        adjoint = ice * (adjoint + omega * (source - image) / diagonal)
    gradient = -friction * ice * (basal_velocity[0] * adjoint[0, LAYERS - 1] + basal_velocity[1] * adjoint[1, LAYERS - 1])
    return adjoint, gradient
```

```python
import functools
import math

import jax
import jax.numpy as jnp
from jax import lax
from jax.experimental import pallas as pl
from jax.experimental.pallas import tpu as pltpu
from jax.sharding import PartitionSpec as P

ITERS = 3
GX = 8
GY = 16
TILES = GX * GY
CAP = 16
SB = 1024
LAYERS = 20
TX = 64
TY = 128
BASE = 16
ROWS = 96
F32 = jnp.float32
BF16 = jnp.bfloat16
MESH = pl.DeviceIdType.MESH
SIDES = ((0, -1), (0, 1), (-1, 0), (1, 0), (-1, -1), (-1, 1), (1, -1), (1, 1))


def omega_list(count):
    return [1.0 / (1.3 + 1.2 * math.cos((2 * k + 1) * math.pi / (2 * count))) for k in range(count)]


def lanes():
    return lax.broadcasted_iota(jnp.int32, (8, 128), 1)


def roll(x, shift):
    return pltpu.roll(x, shift, 1)


def four_n(e, f, o, heavy_x):
    exm, exp_, eym, eyp = e
    fxm, fxp, fym, fyp = f
    dym, dyp, dxm, dxp = o
    if heavy_x:
        x = exm * (4.0 * fxm - dym) + exp_ * (4.0 * fxp + dyp)
        y = eym * (2.0 * fym - dxm) + eyp * (2.0 * fyp + dxp)
        return 2.0 * x + y, 8.0 * (fxm + fxp), 2.0 * (fym + fyp)
    x = exm * (2.0 * fxm - dym) + exp_ * (2.0 * fxp + dyp)
    y = eym * (4.0 * fym - dxm) + eyp * (4.0 * fyp + dxp)
    return x + 2.0 * y, 2.0 * (fxm + fxp), 8.0 * (fym + fyp)


def kernel(
    adj_hbm, eta_hbm, fric_hbm, ice_hbm, mis_hbm, tile_hbm, row_hbm,
    out_ref, c3_ref,
    fa, fb, et, eym, eyp, gu, gv, icef, frip,
    e_own, e_left, e_right, pr, rr, s0, s1, s2, se, sg, ymv, ypv,
    tile_v, row_v, slot_v, mis_v, mis_f, vals, sendb, recvb, rsend, rrecv, surf,
    c1, c2, ec, tc1, tc2, te, tg, ycm, ycp,
    in_sem, a_send, a_recv, r_send, r_recv, h_send, h_recv, q_send, q_recv, c_send, c_recv, bar2,
):
    me_x = lax.axis_index("gx")
    me_y = lax.axis_index("gy")
    me = me_x * GY + me_y
    omegas = omega_list(ITERS)

    def at(dx, dy):
        return (lax.rem(me_x + dx + GX, GX), lax.rem(me_y + dy + GY, GY))

    ins = [
        (tile_hbm, tile_v), (row_hbm, row_v), (mis_hbm, mis_v),
        (ice_hbm, icef.at[pl.ds(BASE, TX)]), (fric_hbm, frip.at[pl.ds(BASE, TX)]),
        (eta_hbm, et.at[pl.ds(1, LAYERS), pl.ds(BASE, TX)]),
        (adj_hbm, fa.at[:, pl.ds(1, LAYERS), pl.ds(BASE, TX)]),
    ]
    loads = [pltpu.make_async_copy(s, d, in_sem.at[i]) for i, (s, d) in enumerate(ins)]
    for c in loads:
        c.start()
    barrier = pltpu.get_barrier_semaphore()
    for k in range(1, GY):
        pl.semaphore_signal(barrier, inc=1, device_id=at(0, k), device_id_type=MESH)
    for k in range(1, GX):
        pl.semaphore_signal(barrier, inc=1, device_id=at(k, 0), device_id_type=MESH)

    loads[0].wait()
    loads[1].wait()
    ii = lax.broadcasted_iota(jnp.int32, (256, 512), 0)
    jj = lax.broadcasted_iota(jnp.int32, (256, 512), 1)
    tri = jnp.where((ii < jj) | (jj >= 256), 1.0, 0.0).astype(BF16)
    tsub = lax.broadcasted_iota(jnp.int32, (TILES, 256), 0)
    running = jnp.zeros((TILES, 256), F32)
    rmat = jnp.zeros((TILES, 128), F32)
    for c in range(4):
        t = tile_v[:, pl.ds(256 * c, 256)]
        hit = jnp.where(t == tsub, 1.0, 0.0)
        hot = hit.astype(BF16)
        sums = jnp.dot(hot, tri, preferred_element_type=F32)
        pos = jnp.sum(hit * (running + sums[:, :256]), axis=0, keepdims=True)
        running = running + sums[:, 256:]
        slot_v[:, pl.ds(256 * c, 256)] = t.astype(F32) * float(CAP) + pos
        z = jnp.where(
            pos == (tsub & (CAP - 1)).astype(F32), row_v[:, pl.ds(256 * c, 256)].astype(F32) + 1.0, 0.0
        ).astype(BF16)
        rmat = rmat + lax.dot_general(hot, z, (((1,), (1,)), ((), ())), preferred_element_type=F32)
    rsend[...] = rmat.reshape(TILES, 1, 128)

    pl.semaphore_wait(barrier, GX + GY - 2)
    for k in range(1, GX):
        pl.semaphore_signal(bar2, inc=1, device_id=at(k, 0), device_id_type=MESH)

    for c in loads[3:]:
        c.wait()
    lane = lanes()

    def build(rb, carry):
        r = pl.multiple_of(BASE + rb * 8, 8)
        q = pl.multiple_of(8 + rb * 8, 8)
        ice = icef[pl.ds(r, 8)]
        edge = jnp.zeros((8, 128), F32)

        def put(acc, x, unit):
            return jnp.where((lane >= 8 * unit) & (lane < 8 * unit + 8), roll(x, (8 * unit + 4) % 128), acc)

        for kind in range(3):
            acc = jnp.zeros((8, 128), F32)
            for l in range(LAYERS):
                if kind < 2:
                    x = ice * fa[kind, l + 1, pl.ds(r, 8)]
                    fa[kind, l + 1, pl.ds(r, 8)] = x
                else:
                    x = et[l + 1, pl.ds(r, 8)]
                if l < 16:
                    acc = put(acc, x, l)
                else:
                    edge = put(edge, x, 4 * kind + l - 16)
            e_own[kind, pl.ds(q, 8)] = acc
        edge = put(edge, ice, 12)
        edge = put(edge, frip[pl.ds(r, 8)], 13)
        e_own[3, pl.ds(q, 8)] = edge
        return carry

    lax.fori_loop(0, 8, build, 0)

    def pack_rows(l, carry):
        for up in range(2):
            r = BASE + (TX - 4) * up
            pr[up, l] = fa[0, l + 1, pl.ds(r, 4)]
            pr[up, LAYERS + l] = fa[1, l + 1, pl.ds(r, 4)]
            pr[up, 2 * LAYERS + l] = et[l + 1, pl.ds(r, 4)]
        return carry

    lax.fori_loop(0, LAYERS, pack_rows, 0)
    for up in range(2):
        r = BASE + (TX - 4) * up
        pr[up, 3 * LAYERS] = icef[pl.ds(r, 4)]
        pr[up, 3 * LAYERS + 1] = frip[pl.ds(r, 4)]

    pl.semaphore_wait(bar2, GX - 1)

    def span(dx):
        if dx == 0:
            return pl.ds(8, TX), pl.ds(8, TX)
        return (pl.ds(8, 8), pl.ds(72, 8)) if dx < 0 else (pl.ds(64, 8), pl.ds(0, 8))

    halos = []
    for i, (dx, dy) in enumerate(SIDES):
        src, dst = span(dx)
        land = (e_right, e_own, e_left)[dy + 1]
        halos.append(
            pltpu.make_async_remote_copy(
                e_own.at[:, src], land.at[:, dst], h_send.at[i], h_recv.at[i],
                device_id=at(dx, dy), device_id_type=MESH,
            )
        )
    for up, dx in ((0, -1), (1, 1)):
        halos.append(
            pltpu.make_async_remote_copy(
                pr.at[up], rr.at[1 - up], q_send.at[up], q_recv.at[up], device_id=at(dx, 0), device_id_type=MESH
            )
        )
    for c in halos:
        c.start()

    loads[2].wait()

    def widen(i, carry):
        mis_f[pl.ds(pl.multiple_of(i * 128, 128), 128)] = mis_v[pl.ds(pl.multiple_of(i * 128, 128), 128)].astype(F32)
        return carry

    lax.fori_loop(0, 16, widen, 0)
    for c in range(2):
        for i in range(8):
            vals[pl.ds(128 * i, 128), pl.ds(128 * c, 128)] = mis_f[pl.ds(256 * i + c, 128, stride=2)].astype(BF16)

    own_values = pltpu.make_async_copy(sendb.at[me], recvb.at[me], a_recv.at[0])
    own_rows = pltpu.make_async_copy(rsend.at[me], rrecv.at[me], r_recv.at[0])
    own_rows.start()

    def pack(j, carry):
        px = lax.rem(me_x + j, GX)
        want = (px * (GY * CAP)).astype(F32) + lax.broadcasted_iota(jnp.int32, (256, SB), 0).astype(F32)
        sel = jnp.where(slot_v[...] == want, 1.0, 0.0).astype(BF16)
        got = jnp.dot(sel, vals[...], preferred_element_type=F32).astype(BF16)
        sendb[pl.ds(px * GY, GY)] = got.reshape(GY, CAP, 2 * TY)

        def send(k, inner):
            py = lax.rem(me_y + k, GY)
            d = px * GY + py
            pltpu.make_async_remote_copy(
                sendb.at[d], recvb.at[me], a_send, a_recv.at[j], device_id=(px, py), device_id_type=MESH
            ).start()
            pltpu.make_async_remote_copy(
                rsend.at[d], rrecv.at[me], r_send, r_recv.at[j], device_id=(px, py), device_id_type=MESH
            ).start()
            return inner

        lax.fori_loop(jnp.where(j == 0, 1, 0), GY, send, 0)
        return carry

    lax.fori_loop(0, GX, pack, 0)
    own_values.start()

    zero = jnp.zeros((8, 128), F32)

    def clear(r, carry):
        q = pl.ds(pl.multiple_of(r * 8, 8), 8)
        for end in (0, LAYERS + 1):
            et[end, q] = zero
            for c in range(2):
                fa[c, end, q] = zero
                fb[c, end, q] = zero
        return carry

    lax.fori_loop(0, ROWS // 8, clear, 0)

    def flag(cond):
        return jnp.where(cond, 1.0, 0.0).astype(F32)

    has_up, has_down = flag(me_x > 0), flag(me_x < GX - 1)
    has_left, has_right = flag(me_y > 0), flag(me_y < GY - 1)
    for c in halos:
        c.wait()

    def unpack_rows(l, carry):
        for side, r, has in ((0, BASE - 4, has_up), (1, BASE + TX, has_down)):
            fa[0, l + 1, pl.ds(r, 4)] = rr[side, l] * has
            fa[1, l + 1, pl.ds(r, 4)] = rr[side, LAYERS + l] * has
            et[l + 1, pl.ds(r, 4)] = rr[side, 2 * LAYERS + l] * has
        return carry

    lax.fori_loop(0, LAYERS, unpack_rows, 0)
    for side, r, has in ((0, BASE - 4, has_up), (1, BASE + TX, has_down)):
        icef[pl.ds(r, 4)] = rr[side, 3 * LAYERS] * has
        frip[pl.ds(r, 4)] = rr[side, 3 * LAYERS + 1] * has

    low4 = (lane & 7) < 4

    def tile_units(x):
        x = jnp.where(lane < 8, x, 0.0)
        for s in (8, 16, 32, 64):
            x = x + roll(x, s)
        return x

    for b in range(10):
        q = pl.ds(8 * b, 8)
        w = pl.ds(8 + 8 * b, 8)
        has = has_up if b == 0 else (has_down if b == 9 else 1.0)
        for side in range(2):
            parts = []
            for kind in range(4):
                own = e_own[kind, q] * has
                if side == 0:
                    parts.append(jnp.where(low4, own, e_right[kind, q] * (has * has_right)))
                else:
                    parts.append(jnp.where(low4, e_left[kind, q] * (has * has_left), own))
            mixed = parts[3]
            first = lane < 32
            s0[0, side, 0, w] = parts[0]
            s0[1, side, 0, w] = parts[1]
            se[side, 0, w] = parts[2]
            s0[0, side, 1, w] = jnp.where(first, mixed, 0.0)
            s0[1, side, 1, w] = jnp.where(first, roll(mixed, 96), 0.0)
            se[side, 1, w] = jnp.where(first, roll(mixed, 64), 0.0)
            sg[side, 0, w] = tile_units(roll(mixed, 32))
            sg[side, 1, w] = jnp.where((lane >= 24) & first, roll(mixed, 48), 0.0)

    def inverse(dx4, dy4, rest, ice):
        du = 4.0 * dx4 + dy4 + rest
        dv = dx4 + 4.0 * dy4 + rest
        live = ice > 0.0
        r = jnp.where(live, 0.25, 0.0) / jnp.where(live, du * dv, 1.0)
        return r * dv, r * du

    def neighbours(x_a, x_b, group):
        if group == 0:
            return (jnp.where(lane < 8, 0.0, roll(x_a, 8)), jnp.where(lane < 120, roll(x_a, 120), roll(x_b, 120)))
        return jnp.where(lane < 8, roll(x_a, 8), roll(x_b, 8)), roll(x_b, 120)

    starts = [14 + 8 * b for b in range(9)]

    def strip_inverse(side, carry):
        for r in starts:
            w = pl.ds(r, 8)
            ice = sg[side, 0, w]
            fric = sg[side, 1, w]
            ea, eb = se[side, 0, w], se[side, 1, w]
            for g, e in ((0, ea), (1, eb)):
                up, down = neighbours(ea, eb, g)
                live = ice if g == 0 else jnp.where(lane < 32, ice, 0.0)
                count = jnp.where((lane < 8) if g == 0 else (lane >= 24), 1.0, 2.0)
                dx4 = 0.5 * (se[side, g, pl.ds(r - 1, 8)] + se[side, g, pl.ds(r + 1, 8)]) + e
                dy4 = 0.5 * (roll(e, 1) + roll(e, 127)) + e
                rest = 2.0 * (up + down + count * e)
                if g == 1:
                    rest = rest + fric
                a, b = inverse(dx4, dy4, rest, live)
                sg[side, 2 + 2 * g, w] = a
                sg[side, 3 + 2 * g, w] = b
        return carry

    lax.fori_loop(0, 2, strip_inverse, 0)

    def shifted(x, left, right):
        return roll(jnp.where(lane == 127, left, x), 1), roll(jnp.where(lane == 0, right, x), 127)

    def main_inverse(l, carry):
        g = l // 16
        unit = l - 16 * g
        lroll, rroll = 124 - 8 * unit, 124 - 8 * unit
        bottom = flag(l == LAYERS - 1)
        count = 2.0 - flag(l == 0) - bottom
        for r in starts:
            w = pl.ds(r, 8)
            e = et[l + 1, w]
            ym, yp = shifted(e, roll(se[1, g, w], lroll), roll(se[0, g, w], rroll))
            eym[l, w] = ym
            eyp[l, w] = yp
            dx4 = 0.5 * (et[l + 1, pl.ds(r - 1, 8)] + et[l + 1, pl.ds(r + 1, 8)]) + e
            dy4 = 0.5 * (ym + yp) + e
            rest = 2.0 * (et[l, w] + et[l + 2, w] + count * e) + bottom * frip[w]
            a, b = inverse(dx4, dy4, rest, icef[w])
            gu[l, w] = a
            gv[l, w] = b
        return carry

    lax.fori_loop(0, LAYERS, main_inverse, 0)

    def strip_sweep(src, dst, omega):
        def one(side, carry):
            for r in starts:
                w, wm, wp = pl.ds(r, 8), pl.ds(r - 1, 8), pl.ds(r + 1, 8)
                ea, eb = se[side, 0, w], se[side, 1, w]
                both = [(src[c, side, 0, w], src[c, side, 1, w]) for c in range(2)]
                for g, e in ((0, ea), (1, eb)):
                    eu, ed = neighbours(ea, eb, g)
                    faces = (se[side, g, wm], se[side, g, wp], roll(e, 1), roll(e, 127))
                    own, diffs = [], []
                    for c in range(2):
                        m, z, p = src[c, side, g, wm], both[c][g], src[c, side, g, wp]
                        own.append((m, p, roll(z, 1), roll(z, 127)))
                        dx = p - m
                        diffs.append((roll(m, 127) - roll(m, 1), roll(p, 127) - roll(p, 1), roll(dx, 1), roll(dx, 127)))
                    for c in range(2):
                        up, down = neighbours(both[c][0], both[c][1], g)
                        total, nx, ny = four_n(faces, own[c], diffs[1 - c], c == 0)
                        total = total + e * (nx + ny + 8.0 * (up + down)) + 8.0 * (eu * up + ed * down)
                        dst[c, side, g, w] = (1.0 - omega) * both[c][g] + omega * (sg[side, 2 + 2 * g + c, w] * total)
            return carry

        lax.fori_loop(0, 2, one, 0)

    def main_sweep(src, strips, omega, rows_at, store):
        def one(l, carry):
            g = l // 16
            unit = l - 16 * g
            lroll, rroll = 124 - 8 * unit, 124 - 8 * unit
            for b in range(1, 11):
                w = pl.ds(8 * b, 8)
                for c in range(2):
                    ym, yp = shifted(
                        src[c, l + 1, w], roll(strips[c, 1, g, w], lroll), roll(strips[c, 0, g, w], rroll)
                    )
                    ymv[c, w] = ym
                    ypv[c, w] = yp
            for r in rows_at:
                w, wm, wp = pl.ds(r, 8), pl.ds(r - 1, 8), pl.ds(r + 1, 8)
                e, eu, ed = et[l + 1, w], et[l, w], et[l + 2, w]
                faces = (et[l + 1, wm], et[l + 1, wp], eym[l, w], eyp[l, w])
                own, diffs = [], []
                for c in range(2):
                    own.append((src[c, l + 1, wm], src[c, l + 1, wp], ymv[c, w], ypv[c, w]))
                    mm, mp, pm, pp = ymv[c, wm], ypv[c, wm], ymv[c, wp], ypv[c, wp]
                    diffs.append((mp - mm, pp - pm, pm - mm, pp - mp))
                for c in range(2):
                    up, down = src[c, l, w], src[c, l + 2, w]
                    total, nx, ny = four_n(faces, own[c], diffs[1 - c], c == 0)
                    total = total + e * (nx + ny + 8.0 * (up + down)) + 8.0 * (eu * up + ed * down)
                    inv = (gu, gv)[c][l, w]
                    store(c, l, r, (1.0 - omega) * src[c, l + 1, w] + omega * (inv * total))
            return carry

        lax.fori_loop(0, LAYERS, one, 0)

    def store_to(dst):
        def store(c, l, r, x):
            dst[c, l + 1, pl.ds(r, 8)] = x

        return store

    def store_out(c, l, r, x):
        out_ref[c, l, pl.ds(r - BASE, 8)] = x

    main_sweep(fa, s0, omegas[0], starts, store_to(fb))
    strip_sweep(s0, s1, omegas[0])
    main_sweep(fb, s1, omegas[1], starts, store_to(fa))
    strip_sweep(s1, s2, omegas[1])

    group = lane // CAP
    sub8 = lax.broadcasted_iota(jnp.int32, (8, 128), 0)
    sub64 = lax.broadcasted_iota(jnp.int32, (TX, 256), 0).astype(F32) + 1.0
    surf[...] = jnp.zeros((TX, 2 * TY), F32)

    def scatter(j, carry):
        sx = lax.rem(me_x - j + GX, GX)
        here = pl.ds(sx * GY, GY)
        pltpu.make_async_copy(recvb.at[here], recvb.at[here], a_recv.at[j]).wait()
        pltpu.make_async_copy(rrecv.at[here], rrecv.at[here], r_recv.at[j]).wait()
        rows = rrecv[here].reshape(GY, 128)
        parts = [
            jnp.sum(jnp.where(sub8 == group, rows[8 * h : 8 * h + 8], 0.0), axis=0, keepdims=True) for h in range(2)
        ]
        hot = jnp.where(jnp.concatenate(parts, axis=1) == sub64, 1.0, 0.0).astype(BF16)
        surf[...] += jnp.dot(hot, recvb[here].reshape(GY * CAP, 2 * TY), preferred_element_type=F32)
        return carry

    lax.fori_loop(0, GX, scatter, 0)

    for b in range(8):
        w = pl.ds(BASE + 8 * b, 8)
        cu = (4.0 * omegas[0]) * (gu[0, w] * surf[pl.ds(8 * b, 8), pl.ds(0, 128)])
        cv = (4.0 * omegas[0]) * (gv[0, w] * surf[pl.ds(8 * b, 8), pl.ds(128, 128)])
        c1[0, w] = cu
        c1[1, w] = cv
        ec[1, w] = jnp.where(lane < 8, roll(cu, 4), roll(cv, 12))

    def span_c(dx):
        if dx == 0:
            return pl.ds(BASE, TX), pl.ds(BASE, TX)
        if dx < 0:
            return pl.ds(BASE, 8), pl.ds(BASE + TX, 8)
        return pl.ds(BASE + TX - 8, 8), pl.ds(BASE - 8, 8)

    edges = []
    for i, (dx, dy) in enumerate(SIDES):
        src, dst = span_c(dx)
        edges.append(
            pltpu.make_async_remote_copy(
                ec.at[1, src], ec.at[1 - dy, dst], c_send.at[i], c_recv.at[i],
                device_id=at(dx, dy), device_id_type=MESH,
            )
        )
    for up, dx in ((0, -1), (1, 1)):
        src, dst = span_c(dx)
        edges.append(
            pltpu.make_async_remote_copy(
                c1.at[:, src], c1.at[:, dst], c_send.at[8 + up], c_recv.at[8 + up],
                device_id=at(dx, 0), device_id_type=MESH,
            )
        )
    for c in edges:
        c.start()

    main_sweep(fa, s2, omegas[2], [BASE + 8 * b for b in range(8)], store_out)
    right = lane < 64

    def join(a, b):
        return jnp.where(right, a, roll(b, 64))

    for r in starts:
        for wr in (r,):
            w = pl.ds(wr, 8)
            te[1, w] = join(roll(se[0, 0, w], 120), roll(se[1, 0, w], 120))
            for c in range(2):
                a, b = sg[0, 2 + c, w], sg[1, 2 + c, w]
                tg[0, c, w] = join(a, b)
                tg[1, c, w] = join(roll(a, 120), roll(b, 120))
    for b in range(1, 11):
        w = pl.ds(8 * b, 8)
        te[0, w] = join(se[0, 0, w], se[1, 0, w])

    for c in edges:
        c.wait()

    for b in range(1, 11):
        w = pl.ds(8 * b, 8)
        has = has_up if b == 1 else (has_down if b == 10 else 1.0)
        own, lef, rig = ec[1, w] * has, ec[0, w] * (has * has_left), ec[2, w] * (has * has_right)
        r_, l_ = jnp.where(low4, own, rig), jnp.where(low4, lef, own)
        tc1[0, w] = join(r_, l_)
        tc1[1, w] = join(roll(r_, 120), roll(l_, 120))
    for w, has in ((pl.ds(BASE - 8, 8), has_up), (pl.ds(BASE + TX, 8), has_down)):
        for c in range(2):
            c1[c, w] = c1[c, w] * has

    w1, w2 = omegas[1], omegas[2]
    again1 = 1.0 - w1 + w1 / omegas[0]
    for r in starts:
        w, wm, wp = pl.ds(r, 8), pl.ds(r - 1, 8), pl.ds(r + 1, 8)
        e = te[0, w]
        faces = (te[0, wm], te[0, wp], roll(e, 1), roll(e, 127))
        own, diffs, mid = [], [], []
        for c in range(2):
            m, z, p = tc1[c, wm], tc1[c, w], tc1[c, wp]
            mid.append(z)
            own.append((m, p, roll(z, 1), roll(z, 127)))
            dx = p - m
            diffs.append((roll(m, 127) - roll(m, 1), roll(p, 127) - roll(p, 1), roll(dx, 1), roll(dx, 127)))
        for c in range(2):
            total, nx, ny = four_n(faces, own[c], diffs[1 - c], c == 0)
            tc2[0, c, w] = again1 * mid[c] + w1 * (tg[0, c, w] * (total + e * (nx + ny)))
            tc2[1, c, w] = (8.0 * w1) * (tg[1, c, w] * ((e + te[1, w]) * mid[c]))

    def shift_all(src, strip, slot):
        for b in range(1, 11):
            w = pl.ds(8 * b, 8)
            for c in range(2):
                t = strip(c, w)
                ym, yp = shifted(src(c, w), roll(t, 60), roll(t, 124))
                ycm[slot, c, w] = ym
                ycp[slot, c, w] = yp

    def around(src, slot, l, w, wm, wp):
        e = et[l + 1, w]
        faces = (et[l + 1, wm], et[l + 1, wp], eym[l, w], eyp[l, w])
        own, diffs = [], []
        for c in range(2):
            own.append((src(c, wm), src(c, wp), ycm[slot, c, w], ycp[slot, c, w]))
            mm, mp, pm, pp = ycm[slot, c, wm], ycp[slot, c, wm], ycm[slot, c, wp], ycp[slot, c, wp]
            diffs.append((mp - mm, pp - pm, pm - mm, pp - mp))
        sums = []
        for c in range(2):
            total, nx, ny = four_n(faces, own[c], diffs[1 - c], c == 0)
            sums.append(total + e * (nx + ny))
        return sums

    shift_all(lambda c, w: c1[c, w], lambda c, w: tc1[c, w], 0)
    for r in starts:
        w, wm, wp = pl.ds(r, 8), pl.ds(r - 1, 8), pl.ds(r + 1, 8)
        sums = around(lambda c, x: c1[c, x], 0, 0, w, wm, wp)
        pair = et[1, w] + et[2, w]
        for c in range(2):
            z = c1[c, w]
            c2[0, c, w] = again1 * z + w1 * ((gu, gv)[c][0, w] * sums[c])
            c2[1, c, w] = (8.0 * w1) * ((gu, gv)[c][1, w] * (pair * z))
    for l in range(2):
        shift_all(lambda c, w: c2[l, c, w], lambda c, w: tc2[l, c, w], l)
    for b in range(8):
        r = BASE + 8 * b
        w, wm, wp = pl.ds(r, 8), pl.ds(r - 1, 8), pl.ds(r + 1, 8)
        pair = 8.0 * (et[1, w] + et[2, w])
        next_pair = (8.0 * w2) * (et[2, w] + et[3, w])
        for l in range(2):
            sums = around(lambda c, x: c2[l, c, x], l, l, w, wm, wp)
            for c in range(2):
                total = sums[c] + pair * c2[1 - l, c, w]
                x = (1.0 - w2) * c2[l, c, w] + w2 * ((gu, gv)[c][l, w] * total)
                c3_ref[c, l, pl.ds(8 * b, 8)] = x + (w2 / omegas[0]) * c1[c, w] if l == 0 else x
        for c in range(2):
            c3_ref[c, 2, pl.ds(8 * b, 8)] = (gu, gv)[c][2, w] * (next_pair * c2[1, c, w])

    pltpu.make_async_copy(sendb.at[pl.ds(0, TILES - 1)], sendb.at[pl.ds(0, TILES - 1)], a_send).wait()
    pltpu.make_async_copy(rsend.at[pl.ds(0, TILES - 1)], rsend.at[pl.ds(0, TILES - 1)], r_send).wait()


def padded(*lead):
    return pltpu.VMEM((*lead, ROWS, TY), F32)


def on_device(adjoint_prev, viscosity, friction, basal_velocity, ice_mask, misfit, block_tile, block_row):
    ice = ice_mask.astype(F32)
    hbm = pl.BlockSpec(memory_space=pltpu.HBM)
    vmem = pl.BlockSpec(memory_space=pltpu.VMEM)
    dma = pltpu.SemaphoreType.DMA
    base, corr = pl.pallas_call(
        kernel,
        out_shape=(
            jax.ShapeDtypeStruct((2, LAYERS, TX, TY), F32),
            jax.ShapeDtypeStruct((2, 3, TX, TY), F32),
        ),
        in_specs=[hbm] * 7,
        out_specs=(vmem, vmem),
        scratch_shapes=[
            padded(2, LAYERS + 2), padded(2, LAYERS + 2), padded(LAYERS + 2),
            padded(LAYERS), padded(LAYERS), padded(LAYERS), padded(LAYERS),
            padded(), padded(),
            pltpu.VMEM((4, 80, 128), F32), pltpu.VMEM((4, 80, 128), F32), pltpu.VMEM((4, 80, 128), F32),
            pltpu.VMEM((2, 62, 4, 128), F32), pltpu.VMEM((2, 62, 4, 128), F32),
            padded(2, 2, 2), padded(2, 2, 2), padded(2, 2, 2), padded(2, 2), padded(2, 6),
            padded(2), padded(2),
            pltpu.VMEM((1, SB), jnp.int32), pltpu.VMEM((1, SB), jnp.int32), pltpu.VMEM((1, SB), F32),
            pltpu.VMEM((2 * SB, TY), BF16), pltpu.VMEM((2 * SB, TY), F32), pltpu.VMEM((SB, 2 * TY), BF16),
            pltpu.VMEM((TILES, CAP, 2 * TY), BF16), pltpu.VMEM((TILES, CAP, 2 * TY), BF16),
            pltpu.VMEM((TILES, 1, 128), F32), pltpu.VMEM((TILES, 1, 128), F32),
            pltpu.VMEM((TX, 2 * TY), F32),
            padded(2), padded(2, 2), padded(3), padded(2), padded(2, 2),
            padded(2), padded(2, 2), padded(2, 2), padded(2, 2),
            dma((7,)), dma, dma((GX,)), dma, dma((GX,)),
            dma((8,)), dma((8,)), dma((2,)), dma((2,)), dma((10,)), dma((10,)),
            pltpu.SemaphoreType.REGULAR,
        ],
        compiler_params=pltpu.CompilerParams(
            collective_id=0, has_side_effects=True, vmem_limit_bytes=48 * 2**20
        ),
    )(
        adjoint_prev, viscosity, friction, ice,
        misfit.reshape(2 * SB, TY), block_tile.reshape(1, SB), block_row.reshape(1, SB),
    )
    adjoint = base + jnp.pad(corr, ((0, 0), (0, LAYERS - 3), (0, 0), (0, 0)))
    gradient = -friction * ice * (basal_velocity[0] * base[0, LAYERS - 1] + basal_velocity[1] * base[1, LAYERS - 1])
    return adjoint, gradient


def solution(mesh):
    placed = (
        P(None, None, "gx", "gy"),
        P(None, "gx", "gy"),
        P("gx", "gy"),
        P(None, "gx", "gy"),
        P("gx", "gy"),
        P(("gx", "gy"), None, None),
        P(("gx", "gy"), None),
        P(("gx", "gy")),
    )
    return jax.shard_map(
        on_device,
        mesh=mesh,
        in_specs=placed,
        out_specs=(P(None, None, "gx", "gy"), P("gx", "gy")),
        check_vma=False,
    )
```

```python
import functools
import math

import jax
import jax.numpy as jnp
from jax import lax
from jax.experimental import pallas as pl
from jax.experimental.pallas import tpu as pltpu
from jax.sharding import PartitionSpec as P

ITERS = 3
GX = 8
GY = 16
TILES = GX * GY
CAP = 16
SB = 1024
LAYERS = 20
TX = 64
TY = 128
BASE = 16
ROWS = 96
F32 = jnp.float32
BF16 = jnp.bfloat16
MESH = pl.DeviceIdType.MESH
SIDES = ((0, -1), (0, 1), (-1, 0), (1, 0), (-1, -1), (-1, 1), (1, -1), (1, 1))


def omega_list(count):
    return [1.0 / (1.3 + 1.2 * math.cos((2 * k + 1) * math.pi / (2 * count))) for k in range(count)]


def lanes():
    return lax.broadcasted_iota(jnp.int32, (8, 128), 1)


def roll(x, shift):
    return pltpu.roll(x, shift, 1)


def four_n(e, f, o, heavy_x):
    exm, exp_, eym, eyp = e
    fxm, fxp, fym, fyp = f
    dym, dyp, dxm, dxp = o
    if heavy_x:
        x = exm * (4.0 * fxm - dym) + exp_ * (4.0 * fxp + dyp)
        y = eym * (2.0 * fym - dxm) + eyp * (2.0 * fyp + dxp)
        return 2.0 * x + y, 8.0 * (fxm + fxp), 2.0 * (fym + fyp)
    x = exm * (2.0 * fxm - dym) + exp_ * (2.0 * fxp + dyp)
    y = eym * (4.0 * fym - dxm) + eyp * (4.0 * fyp + dxp)
    return x + 2.0 * y, 2.0 * (fxm + fxp), 8.0 * (fym + fyp)


def kernel(
    adj_hbm, eta_hbm, fric_hbm, vel_hbm, ice_hbm, mis_hbm, tile_hbm, row_hbm,
    out_hbm, grad_hbm,
    fa, fb, et, eym, eyp, gu, gv, icei, icef, frip,
    e_own, e_left, e_right, pr, rr, s0, s1, s2, se, si, sf, sg, sn, sym, syp, h0, h1, h2, he, yma, ypa, ymb, ypb,
    vel_v, grad_v, tile_v, row_v, slot_v, mis_v, mis_f, vals, sendb, recvb, rsend, rrecv, surf,
    c1, c2, c3, ec, tc1, tc2, tym, typ, te, tg, ycm, ycp,
    in_sem, a_send, a_recv, r_send, r_recv, h_send, h_recv, q_send, q_recv, c_send, c_recv, o_sem, bar2,
):
    me_x = lax.axis_index("gx")
    me_y = lax.axis_index("gy")
    me = me_x * GY + me_y
    omegas = omega_list(ITERS)

    def at(dx, dy):
        return (lax.rem(me_x + dx + GX, GX), lax.rem(me_y + dy + GY, GY))

    ins = [
        (tile_hbm, tile_v), (row_hbm, row_v), (mis_hbm, mis_v),
        (vel_hbm, vel_v), (ice_hbm, icei), (fric_hbm, frip.at[pl.ds(BASE, TX)]),
        (eta_hbm, et.at[pl.ds(1, LAYERS), pl.ds(BASE, TX)]),
        (adj_hbm, fa.at[:, pl.ds(1, LAYERS), pl.ds(BASE, TX)]),
    ]
    loads = [pltpu.make_async_copy(s, d, in_sem.at[i]) for i, (s, d) in enumerate(ins)]
    for c in loads:
        c.start()
    barrier = pltpu.get_barrier_semaphore()
    for k in range(1, GY):
        pl.semaphore_signal(barrier, inc=1, device_id=at(0, k), device_id_type=MESH)
    for k in range(1, GX):
        pl.semaphore_signal(barrier, inc=1, device_id=at(k, 0), device_id_type=MESH)
    for dx, dy in SIDES[4:]:
        pl.semaphore_signal(barrier, inc=1, device_id=at(dx, dy), device_id_type=MESH)


    for c in loads[4:]:
        c.wait()
    lane = lanes()

    def build(rb, carry):
        r = pl.multiple_of(BASE + rb * 8, 8)
        q = pl.multiple_of(8 + rb * 8, 8)
        ice = icei[pl.ds(pl.multiple_of(rb * 8, 8), 8)].astype(F32)
        icef[pl.ds(r, 8)] = ice
        edge = jnp.zeros((8, 128), F32)

        def put(acc, x, unit):
            return jnp.where((lane >= 8 * unit) & (lane < 8 * unit + 8), roll(x, (8 * unit + 4) % 128), acc)

        for kind in range(3):
            acc = jnp.zeros((8, 128), F32)
            for l in range(LAYERS):
                if kind < 2:
                    x = ice * fa[kind, l + 1, pl.ds(r, 8)]
                    fa[kind, l + 1, pl.ds(r, 8)] = x
                else:
                    x = et[l + 1, pl.ds(r, 8)]
                if l < 16:
                    acc = put(acc, x, l)
                else:
                    edge = put(edge, x, 4 * kind + l - 16)
            e_own[kind, pl.ds(q, 8)] = acc
        edge = put(edge, ice, 12)
        edge = put(edge, frip[pl.ds(r, 8)], 13)
        e_own[3, pl.ds(q, 8)] = edge
        return carry

    lax.fori_loop(0, 8, build, 0)

    def pack_rows(l, carry):
        for up in range(2):
            r = BASE + (TX - 4) * up
            pr[up, l] = fa[0, l + 1, pl.ds(r, 4)]
            pr[up, LAYERS + l] = fa[1, l + 1, pl.ds(r, 4)]
            pr[up, 2 * LAYERS + l] = et[l + 1, pl.ds(r, 4)]
        return carry

    lax.fori_loop(0, LAYERS, pack_rows, 0)
    for up in range(2):
        r = BASE + (TX - 4) * up
        pr[up, 3 * LAYERS] = icef[pl.ds(r, 4)]
        pr[up, 3 * LAYERS + 1] = frip[pl.ds(r, 4)]

    pl.semaphore_wait(barrier, GX + GY + 2)
    for k in range(1, GX):
        pl.semaphore_signal(bar2, inc=1, device_id=at(k, 0), device_id_type=MESH)

    def span(dx):
        if dx == 0:
            return pl.ds(8, TX), pl.ds(8, TX)
        return (pl.ds(8, 8), pl.ds(72, 8)) if dx < 0 else (pl.ds(64, 8), pl.ds(0, 8))

    halos = []
    for i, (dx, dy) in enumerate(SIDES):
        src, dst = span(dx)
        land = (e_right, e_own, e_left)[dy + 1]
        halos.append(
            pltpu.make_async_remote_copy(
                e_own.at[:, src], land.at[:, dst], h_send.at[i], h_recv.at[i],
                device_id=at(dx, dy), device_id_type=MESH,
            )
        )
    for up, dx in ((0, -1), (1, 1)):
        halos.append(
            pltpu.make_async_remote_copy(
                pr.at[up], rr.at[1 - up], q_send.at[up], q_recv.at[up], device_id=at(dx, 0), device_id_type=MESH
            )
        )
    for c in halos:
        c.start()

    loads[0].wait()
    loads[1].wait()
    ii = lax.broadcasted_iota(jnp.int32, (256, 512), 0)
    jj = lax.broadcasted_iota(jnp.int32, (256, 512), 1)
    tri = jnp.where((ii < jj) | (jj >= 256), 1.0, 0.0).astype(BF16)
    tsub = lax.broadcasted_iota(jnp.int32, (TILES, 256), 0)
    running = jnp.zeros((TILES, 256), F32)
    rmat = jnp.zeros((TILES, 128), F32)
    for c in range(4):
        t = tile_v[:, pl.ds(256 * c, 256)]
        hit = jnp.where(t == tsub, 1.0, 0.0)
        hot = hit.astype(BF16)
        sums = jnp.dot(hot, tri, preferred_element_type=F32)
        pos = jnp.sum(hit * (running + sums[:, :256]), axis=0, keepdims=True)
        running = running + sums[:, 256:]
        slot_v[:, pl.ds(256 * c, 256)] = t.astype(F32) * float(CAP) + pos
        z = jnp.where(
            pos == (tsub & (CAP - 1)).astype(F32), row_v[:, pl.ds(256 * c, 256)].astype(F32) + 1.0, 0.0
        ).astype(BF16)
        rmat = rmat + lax.dot_general(hot, z, (((1,), (1,)), ((), ())), preferred_element_type=F32)
    rsend[...] = rmat.reshape(TILES, 1, 128)

    loads[2].wait()

    def widen(i, carry):
        mis_f[pl.ds(pl.multiple_of(i * 128, 128), 128)] = mis_v[pl.ds(pl.multiple_of(i * 128, 128), 128)].astype(F32)
        return carry

    lax.fori_loop(0, 16, widen, 0)
    for c in range(2):
        for i in range(8):
            vals[pl.ds(128 * i, 128), pl.ds(128 * c, 128)] = mis_f[pl.ds(256 * i + c, 128, stride=2)].astype(BF16)

    def pack(px, carry):
        want = (px * (GY * CAP)).astype(F32) + lax.broadcasted_iota(jnp.int32, (256, SB), 0).astype(F32)
        sel = jnp.where(slot_v[...] == want, 1.0, 0.0).astype(BF16)
        got = jnp.dot(sel, vals[...], preferred_element_type=F32).astype(BF16)
        sendb[pl.ds(px * GY, GY)] = got.reshape(GY, CAP, 2 * TY)
        return carry

    lax.fori_loop(0, GX, pack, 0)

    pl.semaphore_wait(bar2, GX - 1)
    own_values = pltpu.make_async_copy(sendb.at[me], recvb.at[me], a_recv.at[0])
    own_rows = pltpu.make_async_copy(rsend.at[me], rrecv.at[me], r_recv.at[0])
    own_values.start()
    own_rows.start()

    def send(j, carry):
        px = lax.rem(me_x + j, GX)

        def one(k, inner):
            py = lax.rem(me_y + k, GY)
            d = px * GY + py
            pltpu.make_async_remote_copy(
                sendb.at[d], recvb.at[me], a_send, a_recv.at[j], device_id=(px, py), device_id_type=MESH
            ).start()
            pltpu.make_async_remote_copy(
                rsend.at[d], rrecv.at[me], r_send, r_recv.at[j], device_id=(px, py), device_id_type=MESH
            ).start()
            return inner

        lax.fori_loop(jnp.where(j == 0, 1, 0), GY, one, 0)
        return carry

    lax.fori_loop(0, GX, send, 0)

    zero = jnp.zeros((8, 128), F32)

    def clear(r, carry):
        q = pl.ds(pl.multiple_of(r * 8, 8), 8)
        for end in (0, LAYERS + 1):
            et[end, q] = zero
            for c in range(2):
                fa[c, end, q] = zero
                fb[c, end, q] = zero
        return carry

    lax.fori_loop(0, ROWS // 8, clear, 0)

    def flag(cond):
        return jnp.where(cond, 1.0, 0.0).astype(F32)

    has_up, has_down = flag(me_x > 0), flag(me_x < GX - 1)
    has_left, has_right = flag(me_y > 0), flag(me_y < GY - 1)
    for c in halos:
        c.wait()

    def unpack_rows(l, carry):
        for side, r, has in ((0, BASE - 4, has_up), (1, BASE + TX, has_down)):
            fa[0, l + 1, pl.ds(r, 4)] = rr[side, l] * has
            fa[1, l + 1, pl.ds(r, 4)] = rr[side, LAYERS + l] * has
            et[l + 1, pl.ds(r, 4)] = rr[side, 2 * LAYERS + l] * has
        return carry

    lax.fori_loop(0, LAYERS, unpack_rows, 0)
    for side, r, has in ((0, BASE - 4, has_up), (1, BASE + TX, has_down)):
        icef[pl.ds(r, 4)] = rr[side, 3 * LAYERS] * has
        frip[pl.ds(r, 4)] = rr[side, 3 * LAYERS + 1] * has

    low4 = (lane & 7) < 4

    def tile_units(x):
        x = jnp.where(lane < 8, x, 0.0)
        for s in (8, 16, 32, 64):
            x = x + roll(x, s)
        return x

    right = lane < 64
    half = (lane & 63) < 32

    def join(a, b):
        return jnp.where(right, a, roll(b, 64))

    def halo(dst, x, w):
        dst[0, w] = jnp.where(low4, x[1], x[0])
        dst[1, w] = jnp.where(low4, roll(x[2], 64), x[2])

    for b in range(10):
        q = pl.ds(8 * b, 8)
        w = pl.ds(8 + 8 * b, 8)
        has = has_up if b == 0 else (has_down if b == 9 else 1.0)
        r_, l_ = [], []
        for kind in range(4):
            own = e_own[kind, q] * has
            r_.append(jnp.where(low4, own, e_right[kind, q] * (has * has_right)))
            l_.append(jnp.where(low4, e_left[kind, q] * (has * has_left), own))
        for c in range(3):
            turn = (0, 96, 64)[c]
            mr, ml = (roll(r_[3], turn), roll(l_[3], turn)) if turn else (r_[3], l_[3])
            x = (r_[c], l_[c], jnp.where(half, join(mr, ml), 0.0))
            for p in range(3):
                if c < 2:
                    s0[c, p, w] = x[p]
                else:
                    se[p, w] = x[p]
            halo((h0.at[0], h0.at[1], he)[c], x, w)
        a, d = tile_units(roll(r_[3], 32)), tile_units(roll(l_[3], 32))
        si[0, w] = a
        si[1, w] = d
        si[2, w] = jnp.where(half, jnp.where(right, a, d), 0.0)
        sf[w] = jnp.where(half & ((lane & 63) >= 24), join(roll(r_[3], 48), roll(l_[3], 48)), 0.0)

    def inverse(dx4, dy4, rest, ice):
        du = 4.0 * dx4 + dy4 + rest
        dv = dx4 + 4.0 * dy4 + rest
        live = ice > 0.0
        r = jnp.where(live, 0.25, 0.0) / jnp.where(live, du * dv, 1.0)
        return r * dv, r * du

    def neighbours(x, p):
        if p < 2:
            return (
                jnp.where(lane < 8, 0.0, roll(x[p], 8)),
                jnp.where(lane < 120, roll(x[p], 120), roll(x[2], 120 if p == 0 else 56)),
            )
        up = jnp.where(right, jnp.where(lane < 8, roll(x[0], 8), roll(x[2], 8)), 0.0)
        return (
            jnp.where(right, up, jnp.where(lane < 72, roll(x[1], 72), roll(x[2], 8))),
            roll(x[2], 120),
        )

    starts = [14 + 8 * b for b in range(9)]

    for r in starts:
        w = pl.ds(r, 8)
        es = [se[p, w] for p in range(3)]
        for p, e in enumerate(es):
            up, down = neighbours(es, p)
            count = jnp.where((lane < 8) if p < 2 else ((lane & 63) >= 24), 1.0, 2.0)
            dx4 = 0.5 * (se[p, pl.ds(r - 1, 8)] + se[p, pl.ds(r + 1, 8)]) + e
            ym, yp = roll(e, 1), roll(e, 127)
            for k, x in enumerate((ym, yp, up, down)):
                sn[k, p, w] = x
            dy4 = 0.5 * (ym + yp) + e
            rest = 2.0 * (up + down + count * e)
            if p == 2:
                rest = rest + sf[w]
            a, b = inverse(dx4, dy4, rest, si[p, w])
            sg[0, p, w] = a
            sg[1, p, w] = b

    def shifted(x, beyond):
        return roll(jnp.where(lane == 127, beyond, x), 1), roll(jnp.where(lane == 0, beyond, x), 127)

    def main_inverse(l):
        g = l // 16
        unit = l - 16 * g
        turn = 124 - 8 * unit
        bottom = flag(l == LAYERS - 1)
        count = 2.0 - flag(l == 0) - bottom
        for r in starts:
            w = pl.ds(r, 8)
            e = et[l + 1, w]
            ym, yp = shifted(e, roll(he[g, w], turn))
            eym[l, w] = ym
            eyp[l, w] = yp
            dx4 = 0.5 * (et[l + 1, pl.ds(r - 1, 8)] + et[l + 1, pl.ds(r + 1, 8)]) + e
            dy4 = 0.5 * (ym + yp) + e
            rest = 2.0 * (et[l, w] + et[l + 2, w] + count * e) + bottom * frip[w]
            a, b = inverse(dx4, dy4, rest, icef[w])
            gu[l, w] = a
            gv[l, w] = b

    def inverses(i, carry):
        for k in range(4):
            main_inverse(4 * i + k)
        return carry

    lax.fori_loop(0, LAYERS // 4, inverses, 0)

    def strip_sweep(src, dst, beyond, omega):
        for b in range(1, 11):
            w = pl.ds(8 * b, 8)
            for c in range(2):
                for p in range(3):
                    x = src[c, p, w]
                    sym[c, p, w] = roll(x, 1)
                    syp[c, p, w] = roll(x, 127)
        for r in starts:
            w, wm, wp = pl.ds(r, 8), pl.ds(r - 1, 8), pl.ds(r + 1, 8)
            mid = [[src[c, p, w] for p in range(3)] for c in range(2)]
            new = [[None] * 3 for _ in range(2)]
            for p in range(3):
                e, eu, ed = se[p, w], sn[2, p, w], sn[3, p, w]
                faces = (se[p, wm], se[p, wp], sn[0, p, w], sn[1, p, w])
                own, diffs = [], []
                for c in range(2):
                    own.append((src[c, p, wm], src[c, p, wp], sym[c, p, w], syp[c, p, w]))
                    mm, mp, pm, pp = sym[c, p, wm], syp[c, p, wm], sym[c, p, wp], syp[c, p, wp]
                    diffs.append((mp - mm, pp - pm, pm - mm, pp - mp))
                for c in range(2):
                    up, down = neighbours(mid[c], p)
                    total, nx, ny = four_n(faces, own[c], diffs[1 - c], c == 0)
                    total = total + e * (nx + ny + 8.0 * (up + down)) + 8.0 * (eu * up + ed * down)
                    new[c][p] = (1.0 - omega) * mid[c][p] + omega * (sg[c, p, w] * total)
                    dst[c, p, w] = new[c][p]
            for c in range(2):
                halo(beyond.at[c], new[c], w)

    def main_sweep(src, beyond, omega, first, rows_at, store):
        def shift(l, ym_, yp_):
            g = l // 16
            turn = 124 - 8 * (l - 16 * g)
            for b in range(9):
                w = pl.ds(first + 8 * b, 8)
                for c in range(2):
                    ym, yp = shifted(src[c, l + 1, w], roll(beyond[c, g, w], turn))
                    ym_[c, w] = ym
                    yp_[c, w] = yp

        def sweep(l, ym_, yp_):
            for r in rows_at:
                w, wm, wp = pl.ds(r, 8), pl.ds(r - 1, 8), pl.ds(r + 1, 8)
                e, eu, ed = et[l + 1, w], et[l, w], et[l + 2, w]
                faces = (et[l + 1, wm], et[l + 1, wp], eym[l, w], eyp[l, w])
                own, diffs = [], []
                for c in range(2):
                    own.append((src[c, l + 1, wm], src[c, l + 1, wp], ym_[c, w], yp_[c, w]))
                    mm, mp, pm, pp = ym_[c, wm], yp_[c, wm], ym_[c, wp], yp_[c, wp]
                    diffs.append((mp - mm, pp - pm, pm - mm, pp - mp))
                for c in range(2):
                    up, down = src[c, l, w], src[c, l + 2, w]
                    total, nx, ny = four_n(faces, own[c], diffs[1 - c], c == 0)
                    total = total + e * (nx + ny + 8.0 * (up + down)) + 8.0 * (eu * up + ed * down)
                    inv = (gu, gv)[c][l, w]
                    store(c, l, r, (1.0 - omega) * src[c, l + 1, w] + omega * (inv * total))

        def pair(i, carry):
            l = 2 * i
            shift(l + 1, ymb, ypb)
            sweep(l, yma, ypa)
            shift(l + 2, yma, ypa)
            sweep(l + 1, ymb, ypb)
            return carry

        shift(0, yma, ypa)
        lax.fori_loop(0, LAYERS // 2, pair, 0)

    def store_to(dst):
        def store(c, l, r, x):
            dst[c, l + 1, pl.ds(r, 8)] = x

        return store

    main_sweep(fa, h0, omegas[0], 13, starts, store_to(fb))
    strip_sweep(s0, s1, h1, omegas[0])
    main_sweep(fb, h1, omegas[1], 14, [15 + 8 * b for b in range(9)], store_to(fa))

    group = lane // CAP
    sub8 = lax.broadcasted_iota(jnp.int32, (8, 128), 0)
    sub64 = lax.broadcasted_iota(jnp.int32, (TX, 256), 0).astype(F32) + 1.0
    for j in range(GX):
        here = pl.ds(lax.rem(me_x - j + GX, GX) * GY, GY)
        pltpu.make_async_copy(recvb.at[here], recvb.at[here], a_recv.at[j]).wait()
        pltpu.make_async_copy(rrecv.at[here], rrecv.at[here], r_recv.at[j]).wait()
    total = jnp.zeros((TX, 2 * TY), F32)
    for j in range(GX):
        rows = rrecv[pl.ds(j * GY, GY)].reshape(GY, 128)
        parts = [
            jnp.sum(jnp.where(sub8 == group, rows[8 * h : 8 * h + 8], 0.0), axis=0, keepdims=True) for h in range(2)
        ]
        hot = jnp.where(jnp.concatenate(parts, axis=1) == sub64, 1.0, 0.0).astype(BF16)
        got = recvb[pl.ds(j * GY, GY)].reshape(GY * CAP, 2 * TY)
        total = total + jnp.dot(hot, got, preferred_element_type=F32)
    surf[...] = total

    for b in range(8):
        w = pl.ds(BASE + 8 * b, 8)
        cu = (4.0 * omegas[0]) * (gu[0, w] * surf[pl.ds(8 * b, 8), pl.ds(0, 128)])
        cv = (4.0 * omegas[0]) * (gv[0, w] * surf[pl.ds(8 * b, 8), pl.ds(128, 128)])
        c1[0, w] = cu
        c1[1, w] = cv
        ec[1, w] = jnp.where(lane < 8, roll(cu, 4), roll(cv, 12))

    def span_c(dx):
        if dx == 0:
            return pl.ds(BASE, TX), pl.ds(BASE, TX)
        if dx < 0:
            return pl.ds(BASE, 8), pl.ds(BASE + TX, 8)
        return pl.ds(BASE + TX - 8, 8), pl.ds(BASE - 8, 8)

    edges = []
    for i, (dx, dy) in enumerate(SIDES):
        src, dst = span_c(dx)
        edges.append(
            pltpu.make_async_remote_copy(
                ec.at[1, src], ec.at[1 - dy, dst], c_send.at[i], c_recv.at[i],
                device_id=at(dx, dy), device_id_type=MESH,
            )
        )
    for up, dx in ((0, -1), (1, 1)):
        src, dst = span_c(dx)
        edges.append(
            pltpu.make_async_remote_copy(
                c1.at[:, src], c1.at[:, dst], c_send.at[8 + up], c_recv.at[8 + up],
                device_id=at(dx, 0), device_id_type=MESH,
            )
        )
    for c in edges:
        c.start()

    strip_sweep(s1, s2, h2, omegas[1])
    main_sweep(fa, h2, omegas[2], 15, [BASE + 8 * b for b in range(8)], store_to(fb))
    kept = pl.ds(4, LAYERS - 3)
    out_low = pltpu.make_async_copy(fb.at[:, kept, pl.ds(BASE, TX)], out_hbm.at[:, pl.ds(3, LAYERS - 3)], o_sem.at[0])
    out_low.start()
    loads[3].wait()
    for b in range(8):
        r, w = pl.ds(8 * b, 8), pl.ds(BASE + 8 * b, 8)
        flow = vel_v[0, r] * fb[0, LAYERS, w] + vel_v[1, r] * fb[1, LAYERS, w]
        grad_v[r] = -frip[w] * icef[w] * flow
    out_grad = pltpu.make_async_copy(grad_v, grad_hbm, o_sem.at[2])
    out_grad.start()
    for r in starts:
        w = pl.ds(r, 8)
        te[1, w] = join(roll(se[0, w], 120), roll(se[1, w], 120))
        for c in range(2):
            a, b = sg[c, 0, w], sg[c, 1, w]
            tg[0, c, w] = join(a, b)
            tg[1, c, w] = join(roll(a, 120), roll(b, 120))
    for b in range(1, 11):
        w = pl.ds(8 * b, 8)
        e = join(se[0, w], se[1, w])
        te[0, w] = e
        te[2, w] = roll(e, 1)
        te[3, w] = roll(e, 127)

    for c in edges:
        c.wait()

    for w, has in ((pl.ds(BASE - 8, 8), has_up), (pl.ds(BASE + TX, 8), has_down)):
        for c in range(2):
            c1[c, w] = c1[c, w] * has
    for b in range(1, 11):
        w = pl.ds(8 * b, 8)
        has = has_up if b == 1 else (has_down if b == 10 else 1.0)
        own, lef, rig = ec[1, w] * has, ec[0, w] * (has * has_left), ec[2, w] * (has * has_right)
        r_, l_, out = jnp.where(low4, own, rig), jnp.where(low4, lef, own), jnp.where(low4, lef, rig)
        for c in range(2):
            ym, yp = shifted(c1[c, w], roll(out, 124 - 8 * c))
            ycm[0, c, w] = ym
            ycp[0, c, w] = yp
            t = jnp.where(right, roll(r_, 120), roll(l_, 56)) if c else join(r_, l_)
            tc1[c, w] = t
            tym[c, w] = roll(t, 1)
            typ[c, w] = roll(t, 127)

    w1, w2 = omegas[1], omegas[2]
    again1 = 1.0 - w1 + w1 / omegas[0]
    for r in starts:
        w, wm, wp = pl.ds(r, 8), pl.ds(r - 1, 8), pl.ds(r + 1, 8)
        e = te[0, w]
        faces = (te[0, wm], te[0, wp], te[2, w], te[3, w])
        own, diffs, mid = [], [], []
        for c in range(2):
            mid.append(tc1[c, w])
            own.append((tc1[c, wm], tc1[c, wp], tym[c, w], typ[c, w]))
            mm, mp, pm, pp = tym[c, wm], typ[c, wm], tym[c, wp], typ[c, wp]
            diffs.append((mp - mm, pp - pm, pm - mm, pp - mp))
        for c in range(2):
            total, nx, ny = four_n(faces, own[c], diffs[1 - c], c == 0)
            tc2[0, c, w] = again1 * mid[c] + w1 * (tg[0, c, w] * (total + e * (nx + ny)))
            tc2[1, c, w] = (8.0 * w1) * (tg[1, c, w] * ((e + te[1, w]) * mid[c]))

    def shift_all(src, strip, slot):
        for b in range(1, 11):
            w = pl.ds(8 * b, 8)
            for c in range(2):
                t = strip(c, w)
                ym, yp = shifted(src(c, w), jnp.where(right, roll(t, 124), roll(t, 60)))
                ycm[slot, c, w] = ym
                ycp[slot, c, w] = yp

    def around(src, slot, l, w, wm, wp):
        e = et[l + 1, w]
        faces = (et[l + 1, wm], et[l + 1, wp], eym[l, w], eyp[l, w])
        own, diffs = [], []
        for c in range(2):
            own.append((src(c, wm), src(c, wp), ycm[slot, c, w], ycp[slot, c, w]))
            mm, mp, pm, pp = ycm[slot, c, wm], ycp[slot, c, wm], ycm[slot, c, wp], ycp[slot, c, wp]
            diffs.append((mp - mm, pp - pm, pm - mm, pp - mp))
        sums = []
        for c in range(2):
            total, nx, ny = four_n(faces, own[c], diffs[1 - c], c == 0)
            sums.append(total + e * (nx + ny))
        return sums

    for r in starts:
        w, wm, wp = pl.ds(r, 8), pl.ds(r - 1, 8), pl.ds(r + 1, 8)
        sums = around(lambda c, x: c1[c, x], 0, 0, w, wm, wp)
        pair = et[1, w] + et[2, w]
        for c in range(2):
            z = c1[c, w]
            c2[0, c, w] = again1 * z + w1 * ((gu, gv)[c][0, w] * sums[c])
            c2[1, c, w] = (8.0 * w1) * ((gu, gv)[c][1, w] * (pair * z))
    for l in range(2):
        shift_all(lambda c, w: c2[l, c, w], lambda c, w: tc2[l, c, w], l)
    for b in range(8):
        r = BASE + 8 * b
        w, wm, wp = pl.ds(r, 8), pl.ds(r - 1, 8), pl.ds(r + 1, 8)
        pair = 8.0 * (et[1, w] + et[2, w])
        next_pair = (8.0 * w2) * (et[2, w] + et[3, w])
        for l in range(2):
            sums = around(lambda c, x: c2[l, c, x], l, l, w, wm, wp)
            for c in range(2):
                total = sums[c] + pair * c2[1 - l, c, w]
                x = (1.0 - w2) * c2[l, c, w] + w2 * ((gu, gv)[c][l, w] * total)
                if l == 0:
                    x = x + (w2 / omegas[0]) * c1[c, w]
                c3[c, l, pl.ds(8 * b, 8)] = fb[c, l + 1, w] + x
        for c in range(2):
            x = (gu, gv)[c][2, w] * (next_pair * c2[1, c, w])
            c3[c, 2, pl.ds(8 * b, 8)] = fb[c, 3, w] + x

    out_high = pltpu.make_async_copy(c3, out_hbm.at[:, pl.ds(0, 3)], o_sem.at[1])
    out_high.start()

    pltpu.make_async_copy(sendb.at[pl.ds(0, TILES - 1)], sendb.at[pl.ds(0, TILES - 1)], a_send).wait()
    pltpu.make_async_copy(rsend.at[pl.ds(0, TILES - 1)], rsend.at[pl.ds(0, TILES - 1)], r_send).wait()
    out_low.wait()
    out_high.wait()
    out_grad.wait()


def hand_on(adj_ref, grad_ref, out_ref, grad_out_ref, held, grad_held, in_sem, out_sem):
    pairs = []
    for c in range(2):
        for k in range(4):
            at = (c, pl.ds(k * (LAYERS // 4), LAYERS // 4))
            pairs.append((adj_ref.at[at], held.at[at], out_ref.at[at]))
    pairs.append((grad_ref, grad_held, grad_out_ref))
    first = [pltpu.make_async_copy(a, b, in_sem.at[i]) for i, (a, b, _) in enumerate(pairs)]
    second = [pltpu.make_async_copy(b, d, out_sem.at[i]) for i, (_, b, d) in enumerate(pairs)]
    for c in first:
        c.start()
    for c, d in zip(first, second):
        c.wait()
        d.start()
    for d in second:
        d.wait()


def padded(*lead):
    return pltpu.VMEM((*lead, ROWS, TY), F32)


def on_device(adjoint_prev, viscosity, friction, basal_velocity, ice_mask, misfit, block_tile, block_row):
    hbm = pl.BlockSpec(memory_space=pltpu.HBM)
    dma = pltpu.SemaphoreType.DMA
    shapes = (jax.ShapeDtypeStruct((2, LAYERS, TX, TY), F32), jax.ShapeDtypeStruct((TX, TY), F32))
    results = pl.pallas_call(
        kernel,
        out_shape=shapes,
        in_specs=[hbm] * 8,
        out_specs=(hbm, hbm),
        scratch_shapes=[
            padded(2, LAYERS + 2), padded(2, LAYERS + 2), padded(LAYERS + 2),
            padded(LAYERS), padded(LAYERS), padded(LAYERS), padded(LAYERS),
            pltpu.VMEM((TX, TY), jnp.int32), padded(), padded(),
            pltpu.VMEM((4, 80, 128), F32), pltpu.VMEM((4, 80, 128), F32), pltpu.VMEM((4, 80, 128), F32),
            pltpu.VMEM((2, 62, 4, 128), F32), pltpu.VMEM((2, 62, 4, 128), F32),
            padded(2, 3), padded(2, 3), padded(2, 3), padded(3), padded(3), padded(), padded(2, 3),
            padded(4, 3), padded(2, 3), padded(2, 3),
            padded(2, 2), padded(2, 2), padded(2, 2), padded(2),
            padded(2), padded(2), padded(2), padded(2),
            pltpu.VMEM((2, TX, TY), F32), pltpu.VMEM((TX, TY), F32),
            pltpu.VMEM((1, SB), jnp.int32), pltpu.VMEM((1, SB), jnp.int32), pltpu.VMEM((1, SB), F32),
            pltpu.VMEM((2 * SB, TY), BF16), pltpu.VMEM((2 * SB, TY), F32), pltpu.VMEM((SB, 2 * TY), BF16),
            pltpu.VMEM((TILES, CAP, 2 * TY), BF16), pltpu.VMEM((TILES, CAP, 2 * TY), BF16),
            pltpu.VMEM((TILES, 1, 128), F32), pltpu.VMEM((TILES, 1, 128), F32),
            pltpu.VMEM((TX, 2 * TY), F32),
            padded(2), padded(2, 2), pltpu.VMEM((2, 3, TX, TY), F32),
            padded(3), padded(2), padded(2, 2), padded(2), padded(2),
            padded(4), padded(2, 2), padded(2, 2), padded(2, 2),
            dma((8,)), dma, dma((GX,)), dma, dma((GX,)),
            dma((8,)), dma((8,)), dma((2,)), dma((2,)), dma((10,)), dma((10,)), dma((3,)),
            pltpu.SemaphoreType.REGULAR,
        ],
        compiler_params=pltpu.CompilerParams(
            collective_id=0, has_side_effects=True, vmem_limit_bytes=60 * 2**20
        ),
    )(
        adjoint_prev, viscosity, friction, basal_velocity, ice_mask,
        misfit.reshape(2 * SB, TY), block_tile.reshape(1, SB), block_row.reshape(1, SB),
    )
    return pl.pallas_call(
        hand_on,
        out_shape=shapes,
        in_specs=[hbm] * 2,
        out_specs=(hbm, hbm),
        scratch_shapes=[pltpu.VMEM((2, LAYERS, TX, TY), F32), pltpu.VMEM((TX, TY), F32), dma((9,)), dma((9,))],
        compiler_params=pltpu.CompilerParams(vmem_limit_bytes=60 * 2**20),
    )(*results)


def solution(mesh):
    placed = (
        P(None, None, "gx", "gy"),
        P(None, "gx", "gy"),
        P("gx", "gy"),
        P(None, "gx", "gy"),
        P("gx", "gy"),
        P(("gx", "gy"), None, None),
        P(("gx", "gy"), None),
        P(("gx", "gy")),
    )
    return jax.shard_map(
        on_device,
        mesh=mesh,
        in_specs=placed,
        out_specs=(P(None, None, "gx", "gy"), P("gx", "gy")),
        check_vma=False,
    )
```

```python
import functools
import math

import jax
import jax.numpy as jnp
from jax import lax
from jax.experimental import pallas as pl
from jax.experimental.pallas import tpu as pltpu
from jax.sharding import PartitionSpec as P

ITERS = 3
GX = 8
GY = 16
TILES = GX * GY
CAP = 16
SB = 1024
LAYERS = 20
TX = 64
TY = 128
BASE = 16
ROWS = 96
F32 = jnp.float32
BF16 = jnp.bfloat16
MESH = pl.DeviceIdType.MESH
SIDES = ((0, -1), (0, 1), (-1, 0), (1, 0), (-1, -1), (-1, 1), (1, -1), (1, 1))


def omega_list(count):
    return [1.0 / (1.3 + 1.2 * math.cos((2 * k + 1) * math.pi / (2 * count))) for k in range(count)]


def lanes():
    return lax.broadcasted_iota(jnp.int32, (8, 128), 1)


def roll(x, shift):
    return pltpu.roll(x, shift, 1)


def two_n(e, f, o, heavy_x):
    exm, exp_, eym, eyp = e
    fxm, fxp, fym, fyp = f
    dym, dyp, dxm, dxp = o
    if heavy_x:
        fxm, fxp = 4.0 * fxm, 4.0 * fxp
        total = exm * (fxm - dym) + exp_ * (fxp + dyp) + (eym * (fym - 0.5 * dxm) + eyp * (fyp + 0.5 * dxp))
    else:
        fym, fyp = 4.0 * fym, 4.0 * fyp
        total = exm * (fxm - 0.5 * dym) + exp_ * (fxp + 0.5 * dyp) + (eym * (fym - dxm) + eyp * (fyp + dxp))
    return total, (fxm + fxp) + (fym + fyp)


def kernel(
    adj_hbm, eta_hbm, fric_hbm, vel_hbm, ice_hbm, mis_hbm, tile_hbm, row_hbm,
    out_hbm, grad_hbm,
    fa, fb, et, eym, eyp, gu, gv, icei, icef, frip,
    e_own, e_left, e_right, pr, rr, s0, s1, s2, se, si, sf, sg, sn, sym, syp, h0, h1, h2, he, yma, ypa, ymb, ypb,
    vel_v, grad_v, tile_v, row_v, slot_v, mis_v, mis_f, vals, sendb, recvb, rsend, rrecv, surf,
    c1, c2, c3, ec, tc1, tc2, tym, typ, te, tg, ycm, ycp,
    in_sem, a_send, a_recv, r_send, r_recv, h_send, h_recv, q_send, q_recv, c_send, c_recv, o_sem, bar2,
):
    me_x = lax.axis_index("gx")
    me_y = lax.axis_index("gy")
    me = me_x * GY + me_y
    omegas = omega_list(ITERS)

    def at(dx, dy):
        return (lax.rem(me_x + dx + GX, GX), lax.rem(me_y + dy + GY, GY))

    ins = [
        (tile_hbm, tile_v), (row_hbm, row_v), (mis_hbm, mis_v),
        (vel_hbm, vel_v), (ice_hbm, icei), (fric_hbm, frip.at[pl.ds(BASE, TX)]),
        (eta_hbm, et.at[pl.ds(1, LAYERS), pl.ds(BASE, TX)]),
        (adj_hbm, fa.at[:, pl.ds(1, LAYERS), pl.ds(BASE, TX)]),
    ]
    loads = [pltpu.make_async_copy(s, d, in_sem.at[i]) for i, (s, d) in enumerate(ins)]
    for c in loads:
        c.start()
    barrier = pltpu.get_barrier_semaphore()
    for k in range(1, GY):
        pl.semaphore_signal(barrier, inc=1, device_id=at(0, k), device_id_type=MESH)
    for k in range(1, GX):
        pl.semaphore_signal(barrier, inc=1, device_id=at(k, 0), device_id_type=MESH)
    for dx, dy in SIDES[4:]:
        pl.semaphore_signal(barrier, inc=1, device_id=at(dx, dy), device_id_type=MESH)


    for c in loads[4:]:
        c.wait()
    lane = lanes()

    def build(rb, carry):
        r = pl.multiple_of(BASE + rb * 8, 8)
        q = pl.multiple_of(8 + rb * 8, 8)
        ice = icei[pl.ds(pl.multiple_of(rb * 8, 8), 8)].astype(F32)
        icef[pl.ds(r, 8)] = ice
        edge = jnp.zeros((8, 128), F32)

        def put(acc, x, unit):
            return jnp.where((lane >= 8 * unit) & (lane < 8 * unit + 8), roll(x, (8 * unit + 4) % 128), acc)

        for kind in range(3):
            acc = jnp.zeros((8, 128), F32)
            for l in range(LAYERS):
                if kind < 2:
                    x = ice * fa[kind, l + 1, pl.ds(r, 8)]
                    fa[kind, l + 1, pl.ds(r, 8)] = x
                else:
                    x = et[l + 1, pl.ds(r, 8)]
                if l < 16:
                    acc = put(acc, x, l)
                else:
                    edge = put(edge, x, 4 * kind + l - 16)
            e_own[kind, pl.ds(q, 8)] = acc
        edge = put(edge, ice, 12)
        edge = put(edge, frip[pl.ds(r, 8)], 13)
        e_own[3, pl.ds(q, 8)] = edge
        return carry

    lax.fori_loop(0, 8, build, 0)

    def pack_rows(l, carry):
        for up in range(2):
            r = BASE + (TX - 4) * up
            pr[up, l] = fa[0, l + 1, pl.ds(r, 4)]
            pr[up, LAYERS + l] = fa[1, l + 1, pl.ds(r, 4)]
            pr[up, 2 * LAYERS + l] = et[l + 1, pl.ds(r, 4)]
        return carry

    lax.fori_loop(0, LAYERS, pack_rows, 0)
    for up in range(2):
        r = BASE + (TX - 4) * up
        pr[up, 3 * LAYERS] = icef[pl.ds(r, 4)]
        pr[up, 3 * LAYERS + 1] = frip[pl.ds(r, 4)]

    pl.semaphore_wait(barrier, GX + GY + 2)
    for k in range(1, GX):
        pl.semaphore_signal(bar2, inc=1, device_id=at(k, 0), device_id_type=MESH)

    def span(dx):
        if dx == 0:
            return pl.ds(8, TX), pl.ds(8, TX)
        return (pl.ds(8, 8), pl.ds(72, 8)) if dx < 0 else (pl.ds(64, 8), pl.ds(0, 8))

    halos = []
    for i, (dx, dy) in enumerate(SIDES):
        src, dst = span(dx)
        land = (e_right, e_own, e_left)[dy + 1]
        halos.append(
            pltpu.make_async_remote_copy(
                e_own.at[:, src], land.at[:, dst], h_send.at[i], h_recv.at[i],
                device_id=at(dx, dy), device_id_type=MESH,
            )
        )
    for up, dx in ((0, -1), (1, 1)):
        halos.append(
            pltpu.make_async_remote_copy(
                pr.at[up], rr.at[1 - up], q_send.at[up], q_recv.at[up], device_id=at(dx, 0), device_id_type=MESH
            )
        )
    for c in halos:
        c.start()

    loads[0].wait()
    loads[1].wait()
    ii = lax.broadcasted_iota(jnp.int32, (256, 512), 0)
    jj = lax.broadcasted_iota(jnp.int32, (256, 512), 1)
    tri = jnp.where((ii < jj) | (jj >= 256), 1.0, 0.0).astype(BF16)
    tsub = lax.broadcasted_iota(jnp.int32, (TILES, 256), 0)
    running = jnp.zeros((TILES, 256), F32)
    rmat = jnp.zeros((TILES, 128), F32)
    for c in range(4):
        t = tile_v[:, pl.ds(256 * c, 256)]
        hit = jnp.where(t == tsub, 1.0, 0.0)
        hot = hit.astype(BF16)
        sums = jnp.dot(hot, tri, preferred_element_type=F32)
        pos = jnp.sum(hit * (running + sums[:, :256]), axis=0, keepdims=True)
        running = running + sums[:, 256:]
        slot_v[:, pl.ds(256 * c, 256)] = t.astype(F32) * float(CAP) + pos
        z = jnp.where(
            pos == (tsub & (CAP - 1)).astype(F32), row_v[:, pl.ds(256 * c, 256)].astype(F32) + 1.0, 0.0
        ).astype(BF16)
        rmat = rmat + lax.dot_general(hot, z, (((1,), (1,)), ((), ())), preferred_element_type=F32)
    rsend[...] = rmat.reshape(TILES, 1, 128)

    loads[2].wait()

    def widen(i, carry):
        mis_f[pl.ds(pl.multiple_of(i * 128, 128), 128)] = mis_v[pl.ds(pl.multiple_of(i * 128, 128), 128)].astype(F32)
        return carry

    lax.fori_loop(0, 16, widen, 0)
    for c in range(2):
        for i in range(8):
            vals[pl.ds(128 * i, 128), pl.ds(128 * c, 128)] = mis_f[pl.ds(256 * i + c, 128, stride=2)].astype(BF16)

    def pack(px, carry):
        want = (px * (GY * CAP)).astype(F32) + lax.broadcasted_iota(jnp.int32, (256, SB), 0).astype(F32)
        sel = jnp.where(slot_v[...] == want, 1.0, 0.0).astype(BF16)
        got = jnp.dot(sel, vals[...], preferred_element_type=F32).astype(BF16)
        sendb[pl.ds(px * GY, GY)] = got.reshape(GY, CAP, 2 * TY)
        return carry

    lax.fori_loop(0, GX, pack, 0)

    pl.semaphore_wait(bar2, GX - 1)
    own_rows = pltpu.make_async_copy(rsend.at[me], rrecv.at[me], r_recv.at[0])
    own_rows.start()

    def send(j, carry):
        px = lax.rem(me_x + j, GX)

        def one(k, inner):
            py = lax.rem(me_y + k, GY)
            d = px * GY + py
            pltpu.make_async_remote_copy(
                rsend.at[d], rrecv.at[me], r_send, r_recv.at[j], device_id=(px, py), device_id_type=MESH
            ).start()
            return inner

        lax.fori_loop(jnp.where(j == 0, 1, 0), GY, one, 0)
        return carry

    lax.fori_loop(0, GX, send, 0)

    own_values = pltpu.make_async_copy(sendb.at[me], recvb.at[me], a_recv.at[0])
    own_values.start()

    def send_values(j, carry):
        px = lax.rem(me_x + j, GX)

        def one(k, inner):
            py = lax.rem(me_y + k, GY)
            d = px * GY + py
            pltpu.make_async_remote_copy(
                sendb.at[d], recvb.at[me], a_send, a_recv.at[j], device_id=(px, py), device_id_type=MESH
            ).start()
            return inner

        lax.fori_loop(jnp.where(j == 0, 1, 0), GY, one, 0)
        return carry

    lax.fori_loop(0, GX, send_values, 0)

    zero = jnp.zeros((8, 128), F32)

    def clear(r, carry):
        q = pl.ds(pl.multiple_of(r * 8, 8), 8)
        for end in (0, LAYERS + 1):
            et[end, q] = zero
            for c in range(2):
                fa[c, end, q] = zero
                fb[c, end, q] = zero
        return carry

    lax.fori_loop(0, ROWS // 8, clear, 0)

    def flag(cond):
        return jnp.where(cond, 1.0, 0.0).astype(F32)

    has_up, has_down = flag(me_x > 0), flag(me_x < GX - 1)
    has_left, has_right = flag(me_y > 0), flag(me_y < GY - 1)
    for c in halos:
        c.wait()

    def unpack_rows(l, carry):
        for side, r, has in ((0, BASE - 4, has_up), (1, BASE + TX, has_down)):
            fa[0, l + 1, pl.ds(r, 4)] = rr[side, l] * has
            fa[1, l + 1, pl.ds(r, 4)] = rr[side, LAYERS + l] * has
            et[l + 1, pl.ds(r, 4)] = rr[side, 2 * LAYERS + l] * has
        return carry

    lax.fori_loop(0, LAYERS, unpack_rows, 0)
    for side, r, has in ((0, BASE - 4, has_up), (1, BASE + TX, has_down)):
        icef[pl.ds(r, 4)] = rr[side, 3 * LAYERS] * has
        frip[pl.ds(r, 4)] = rr[side, 3 * LAYERS + 1] * has

    low4 = (lane & 7) < 4

    def tile_units(x):
        x = jnp.where(lane < 8, x, 0.0)
        for s in (8, 16, 32, 64):
            x = x + roll(x, s)
        return x

    right = lane < 64
    half = (lane & 63) < 32

    def join(a, b):
        return jnp.where(right, a, roll(b, 64))

    def halo(dst, x, w):
        dst[0, w] = jnp.where(low4, x[1], x[0])
        dst[1, w] = jnp.where(low4, roll(x[2], 64), x[2])

    for b in range(10):
        q = pl.ds(8 * b, 8)
        w = pl.ds(8 + 8 * b, 8)
        has = has_up if b == 0 else (has_down if b == 9 else 1.0)
        r_, l_ = [], []
        for kind in range(4):
            own = e_own[kind, q] * has
            r_.append(jnp.where(low4, own, e_right[kind, q] * (has * has_right)))
            l_.append(jnp.where(low4, e_left[kind, q] * (has * has_left), own))
        for c in range(3):
            turn = (0, 96, 64)[c]
            mr, ml = (roll(r_[3], turn), roll(l_[3], turn)) if turn else (r_[3], l_[3])
            x = (r_[c], l_[c], jnp.where(half, join(mr, ml), 0.0))
            for p in range(3):
                if c < 2:
                    s0[c, p, w] = x[p]
                else:
                    se[p, w] = x[p]
            halo((h0.at[0], h0.at[1], he)[c], x, w)
        a, d = tile_units(roll(r_[3], 32)), tile_units(roll(l_[3], 32))
        si[0, w] = a
        si[1, w] = d
        si[2, w] = jnp.where(half, jnp.where(right, a, d), 0.0)
        sf[w] = jnp.where(half & ((lane & 63) >= 24), join(roll(r_[3], 48), roll(l_[3], 48)), 0.0)

    def inverse(dx4, dy4, rest, ice):
        du = 4.0 * dx4 + dy4 + rest
        dv = dx4 + 4.0 * dy4 + rest
        live = ice > 0.0
        r = jnp.where(live, 0.5, 0.0) / jnp.where(live, du * dv, 1.0)
        return r * dv, r * du

    def neighbours(x, p):
        if p < 2:
            return (
                jnp.where(lane < 8, 0.0, roll(x[p], 8)),
                jnp.where(lane < 120, roll(x[p], 120), roll(x[2], 120 if p == 0 else 56)),
            )
        up = jnp.where(right, jnp.where(lane < 8, roll(x[0], 8), roll(x[2], 8)), 0.0)
        return (
            jnp.where(right, up, jnp.where(lane < 72, roll(x[1], 72), roll(x[2], 8))),
            roll(x[2], 120),
        )

    starts = [14 + 8 * b for b in range(9)]

    for r in starts:
        w = pl.ds(r, 8)
        es = [se[p, w] for p in range(3)]
        for p, e in enumerate(es):
            up, down = neighbours(es, p)
            count = jnp.where((lane < 8) if p < 2 else ((lane & 63) >= 24), 1.0, 2.0)
            dx4 = 0.5 * (se[p, pl.ds(r - 1, 8)] + se[p, pl.ds(r + 1, 8)]) + e
            ym, yp = roll(e, 1), roll(e, 127)
            for k, x in enumerate((ym, yp, up, down)):
                sn[k, p, w] = x
            dy4 = 0.5 * (ym + yp) + e
            rest = 2.0 * (up + down + count * e)
            if p == 2:
                rest = rest + sf[w]
            a, b = inverse(dx4, dy4, rest, si[p, w])
            sg[0, p, w] = a
            sg[1, p, w] = b

    def shifted(x, beyond):
        return roll(jnp.where(lane == 127, beyond, x), 1), roll(jnp.where(lane == 0, beyond, x), 127)

    def main_inverse(l):
        g = l // 16
        unit = l - 16 * g
        turn = 124 - 8 * unit
        bottom = flag(l == LAYERS - 1)
        count = 2.0 - flag(l == 0) - bottom
        for r in starts:
            w = pl.ds(r, 8)
            e = et[l + 1, w]
            ym, yp = shifted(e, roll(he[g, w], turn))
            eym[l, w] = ym
            eyp[l, w] = yp
            dx4 = 0.5 * (et[l + 1, pl.ds(r - 1, 8)] + et[l + 1, pl.ds(r + 1, 8)]) + e
            dy4 = 0.5 * (ym + yp) + e
            rest = 2.0 * (et[l, w] + et[l + 2, w] + count * e) + bottom * frip[w]
            a, b = inverse(dx4, dy4, rest, icef[w])
            gu[l, w] = a
            gv[l, w] = b

    def inverses(i, carry):
        for k in range(4):
            main_inverse(4 * i + k)
        return carry

    lax.fori_loop(0, LAYERS // 4, inverses, 0)

    def strip_sweep(src, dst, beyond, omega):
        for b in range(1, 11):
            w = pl.ds(8 * b, 8)
            for c in range(2):
                for p in range(3):
                    x = src[c, p, w]
                    sym[c, p, w] = roll(x, 1)
                    syp[c, p, w] = roll(x, 127)
        for r in starts:
            w, wm, wp = pl.ds(r, 8), pl.ds(r - 1, 8), pl.ds(r + 1, 8)
            mid = [[src[c, p, w] for p in range(3)] for c in range(2)]
            new = [[None] * 3 for _ in range(2)]
            for p in range(3):
                e, eu, ed = se[p, w], sn[2, p, w], sn[3, p, w]
                faces = (se[p, wm], se[p, wp], sn[0, p, w], sn[1, p, w])
                own, diffs = [], []
                for c in range(2):
                    own.append((src[c, p, wm], src[c, p, wp], sym[c, p, w], syp[c, p, w]))
                    mm, mp, pm, pp = sym[c, p, wm], syp[c, p, wm], sym[c, p, wp], syp[c, p, wp]
                    diffs.append((mp - mm, pp - pm, pm - mm, pp - mp))
                for c in range(2):
                    up, down = neighbours(mid[c], p)
                    total, near = two_n(faces, own[c], diffs[1 - c], c == 0)
                    total = total + e * (near + 4.0 * (up + down)) + 4.0 * (eu * up + ed * down)
                    new[c][p] = (1.0 - omega) * mid[c][p] + omega * (sg[c, p, w] * total)
                    dst[c, p, w] = new[c][p]
            for c in range(2):
                halo(beyond.at[c], new[c], w)

    def main_sweep(src, beyond, omega, first, rows_at, store):
        def shift(l, ym_, yp_):
            g = l // 16
            turn = 124 - 8 * (l - 16 * g)
            for b in range(9):
                w = pl.ds(first + 8 * b, 8)
                for c in range(2):
                    ym, yp = shifted(src[c, l + 1, w], roll(beyond[c, g, w], turn))
                    ym_[c, w] = ym
                    yp_[c, w] = yp

        def sweep(l, ym_, yp_):
            for r in rows_at:
                w, wm, wp = pl.ds(r, 8), pl.ds(r - 1, 8), pl.ds(r + 1, 8)
                e, eu, ed = et[l + 1, w], et[l, w], et[l + 2, w]
                faces = (et[l + 1, wm], et[l + 1, wp], eym[l, w], eyp[l, w])
                own, diffs = [], []
                for c in range(2):
                    own.append((src[c, l + 1, wm], src[c, l + 1, wp], ym_[c, w], yp_[c, w]))
                    mm, mp, pm, pp = ym_[c, wm], yp_[c, wm], ym_[c, wp], yp_[c, wp]
                    diffs.append((mp - mm, pp - pm, pm - mm, pp - mp))
                for c in range(2):
                    up, down = src[c, l, w], src[c, l + 2, w]
                    total, near = two_n(faces, own[c], diffs[1 - c], c == 0)
                    total = total + e * (near + 4.0 * (up + down)) + 4.0 * (eu * up + ed * down)
                    inv = (gu, gv)[c][l, w]
                    store(c, l, r, (1.0 - omega) * src[c, l + 1, w] + omega * (inv * total))

        def pair(i, carry):
            l = 2 * i
            shift(l + 1, ymb, ypb)
            sweep(l, yma, ypa)
            shift(l + 2, yma, ypa)
            sweep(l + 1, ymb, ypb)
            return carry

        shift(0, yma, ypa)
        lax.fori_loop(0, LAYERS // 2, pair, 0)

    def store_to(dst):
        def store(c, l, r, x):
            dst[c, l + 1, pl.ds(r, 8)] = x

        return store

    main_sweep(fa, h0, omegas[0], 13, starts, store_to(fb))
    strip_sweep(s0, s1, h1, omegas[0])
    main_sweep(fb, h1, omegas[1], 14, [15 + 8 * b for b in range(9)], store_to(fa))

    group = lane // CAP
    sub8 = lax.broadcasted_iota(jnp.int32, (8, 128), 0)
    sub64 = lax.broadcasted_iota(jnp.int32, (TX, 256), 0).astype(F32) + 1.0
    for j in range(GX):
        here = pl.ds(lax.rem(me_x - j + GX, GX) * GY, GY)
        pltpu.make_async_copy(recvb.at[here], recvb.at[here], a_recv.at[j]).wait()
        pltpu.make_async_copy(rrecv.at[here], rrecv.at[here], r_recv.at[j]).wait()
    total = jnp.zeros((TX, 2 * TY), F32)
    for j in range(GX):
        rows = rrecv[pl.ds(j * GY, GY)].reshape(GY, 128)
        parts = [
            jnp.sum(jnp.where(sub8 == group, rows[8 * h : 8 * h + 8], 0.0), axis=0, keepdims=True) for h in range(2)
        ]
        hot = jnp.where(jnp.concatenate(parts, axis=1) == sub64, 1.0, 0.0).astype(BF16)
        got = recvb[pl.ds(j * GY, GY)].reshape(GY * CAP, 2 * TY)
        total = total + jnp.dot(hot, got, preferred_element_type=F32)
    surf[...] = total

    for b in range(8):
        w = pl.ds(BASE + 8 * b, 8)
        cu = (2.0 * omegas[0]) * (gu[0, w] * surf[pl.ds(8 * b, 8), pl.ds(0, 128)])
        cv = (2.0 * omegas[0]) * (gv[0, w] * surf[pl.ds(8 * b, 8), pl.ds(128, 128)])
        c1[0, w] = cu
        c1[1, w] = cv
        ec[1, w] = jnp.where(lane < 8, roll(cu, 4), roll(cv, 12))

    def span_c(dx):
        if dx == 0:
            return pl.ds(BASE, TX), pl.ds(BASE, TX)
        if dx < 0:
            return pl.ds(BASE, 8), pl.ds(BASE + TX, 8)
        return pl.ds(BASE + TX - 8, 8), pl.ds(BASE - 8, 8)

    edges = []
    for i, (dx, dy) in enumerate(SIDES):
        src, dst = span_c(dx)
        edges.append(
            pltpu.make_async_remote_copy(
                ec.at[1, src], ec.at[1 - dy, dst], c_send.at[i], c_recv.at[i],
                device_id=at(dx, dy), device_id_type=MESH,
            )
        )
    for up, dx in ((0, -1), (1, 1)):
        src, dst = span_c(dx)
        edges.append(
            pltpu.make_async_remote_copy(
                c1.at[:, src], c1.at[:, dst], c_send.at[8 + up], c_recv.at[8 + up],
                device_id=at(dx, 0), device_id_type=MESH,
            )
        )
    for c in edges:
        c.start()

    strip_sweep(s1, s2, h2, omegas[1])
    main_sweep(fa, h2, omegas[2], 15, [BASE + 8 * b for b in range(8)], store_to(fb))
    kept = pl.ds(4, LAYERS - 3)
    out_low = pltpu.make_async_copy(fb.at[:, kept, pl.ds(BASE, TX)], out_hbm.at[:, pl.ds(3, LAYERS - 3)], o_sem.at[0])
    out_low.start()
    loads[3].wait()
    for b in range(8):
        r, w = pl.ds(8 * b, 8), pl.ds(BASE + 8 * b, 8)
        flow = vel_v[0, r] * fb[0, LAYERS, w] + vel_v[1, r] * fb[1, LAYERS, w]
        grad_v[r] = -frip[w] * icef[w] * flow
    out_grad = pltpu.make_async_copy(grad_v, grad_hbm, o_sem.at[2])
    out_grad.start()
    for r in starts:
        w = pl.ds(r, 8)
        te[1, w] = join(roll(se[0, w], 120), roll(se[1, w], 120))
        for c in range(2):
            a, b = sg[c, 0, w], sg[c, 1, w]
            tg[0, c, w] = join(a, b)
            tg[1, c, w] = join(roll(a, 120), roll(b, 120))
    for b in range(1, 11):
        w = pl.ds(8 * b, 8)
        e = join(se[0, w], se[1, w])
        te[0, w] = e
        te[2, w] = roll(e, 1)
        te[3, w] = roll(e, 127)

    for c in edges:
        c.wait()

    for w, has in ((pl.ds(BASE - 8, 8), has_up), (pl.ds(BASE + TX, 8), has_down)):
        for c in range(2):
            c1[c, w] = c1[c, w] * has
    for b in range(1, 11):
        w = pl.ds(8 * b, 8)
        has = has_up if b == 1 else (has_down if b == 10 else 1.0)
        own, lef, rig = ec[1, w] * has, ec[0, w] * (has * has_left), ec[2, w] * (has * has_right)
        r_, l_, out = jnp.where(low4, own, rig), jnp.where(low4, lef, own), jnp.where(low4, lef, rig)
        for c in range(2):
            ym, yp = shifted(c1[c, w], roll(out, 124 - 8 * c))
            ycm[0, c, w] = ym
            ycp[0, c, w] = yp
            t = jnp.where(right, roll(r_, 120), roll(l_, 56)) if c else join(r_, l_)
            tc1[c, w] = t
            tym[c, w] = roll(t, 1)
            typ[c, w] = roll(t, 127)

    w1, w2 = omegas[1], omegas[2]
    again1 = 1.0 - w1 + w1 / omegas[0]
    for r in starts:
        w, wm, wp = pl.ds(r, 8), pl.ds(r - 1, 8), pl.ds(r + 1, 8)
        e = te[0, w]
        faces = (te[0, wm], te[0, wp], te[2, w], te[3, w])
        own, diffs, mid = [], [], []
        for c in range(2):
            mid.append(tc1[c, w])
            own.append((tc1[c, wm], tc1[c, wp], tym[c, w], typ[c, w]))
            mm, mp, pm, pp = tym[c, wm], typ[c, wm], tym[c, wp], typ[c, wp]
            diffs.append((mp - mm, pp - pm, pm - mm, pp - mp))
        for c in range(2):
            total, near = two_n(faces, own[c], diffs[1 - c], c == 0)
            for l, t in enumerate((
                again1 * mid[c] + w1 * (tg[0, c, w] * (total + e * near)),
                (4.0 * w1) * (tg[1, c, w] * ((e + te[1, w]) * mid[c])),
            )):
                tc2[l, c, w] = jnp.where(right, roll(t, 124), roll(t, 60))

    def around(src, slot, l, w, wm, wp):
        e = et[l + 1, w]
        faces = (et[l + 1, wm], et[l + 1, wp], eym[l, w], eyp[l, w])
        own, diffs = [], []
        for c in range(2):
            own.append((src(c, wm), src(c, wp), ycm[slot, c, w], ycp[slot, c, w]))
            mm, mp, pm, pp = ycm[slot, c, wm], ycp[slot, c, wm], ycm[slot, c, wp], ycp[slot, c, wp]
            diffs.append((mp - mm, pp - pm, pm - mm, pp - mp))
        sums = []
        for c in range(2):
            total, near = two_n(faces, own[c], diffs[1 - c], c == 0)
            sums.append(total + e * near)
        return sums

    for r in starts:
        w, wm, wp = pl.ds(r, 8), pl.ds(r - 1, 8), pl.ds(r + 1, 8)
        sums = around(lambda c, x: c1[c, x], 0, 0, w, wm, wp)
        pair = et[1, w] + et[2, w]
        for c in range(2):
            z = c1[c, w]
            for l, x in enumerate((
                again1 * z + w1 * ((gu, gv)[c][0, w] * sums[c]),
                (4.0 * w1) * ((gu, gv)[c][1, w] * (pair * z)),
            )):
                c2[l, c, w] = x
                ym, yp = shifted(x, tc2[l, c, w])
                ycm[1 + l, c, w] = ym
                ycp[1 + l, c, w] = yp
    for b in range(8):
        r = BASE + 8 * b
        w, wm, wp = pl.ds(r, 8), pl.ds(r - 1, 8), pl.ds(r + 1, 8)
        pair = 4.0 * (et[1, w] + et[2, w])
        next_pair = (4.0 * w2) * (et[2, w] + et[3, w])
        for l in range(2):
            sums = around(lambda c, x: c2[l, c, x], 1 + l, l, w, wm, wp)
            for c in range(2):
                total = sums[c] + pair * c2[1 - l, c, w]
                x = (1.0 - w2) * c2[l, c, w] + w2 * ((gu, gv)[c][l, w] * total)
                if l == 0:
                    x = x + (w2 / omegas[0]) * c1[c, w]
                c3[c, l, pl.ds(8 * b, 8)] = fb[c, l + 1, w] + x
        for c in range(2):
            x = (gu, gv)[c][2, w] * (next_pair * c2[1, c, w])
            c3[c, 2, pl.ds(8 * b, 8)] = fb[c, 3, w] + x

    out_high = pltpu.make_async_copy(c3, out_hbm.at[:, pl.ds(0, 3)], o_sem.at[1])
    out_high.start()

    pltpu.make_async_copy(sendb.at[pl.ds(0, TILES - 1)], sendb.at[pl.ds(0, TILES - 1)], a_send).wait()
    pltpu.make_async_copy(rsend.at[pl.ds(0, TILES - 1)], rsend.at[pl.ds(0, TILES - 1)], r_send).wait()
    out_low.wait()
    out_high.wait()
    out_grad.wait()


def hand_on(adj_ref, grad_ref, out_ref, grad_out_ref, held, grad_held, in_sem, out_sem):
    pairs = []
    for c in range(2):
        for k in range(4):
            at = (c, pl.ds(k * (LAYERS // 4), LAYERS // 4))
            pairs.append((adj_ref.at[at], held.at[at], out_ref.at[at]))
    pairs.append((grad_ref, grad_held, grad_out_ref))
    first = [pltpu.make_async_copy(a, b, in_sem.at[i]) for i, (a, b, _) in enumerate(pairs)]
    second = [pltpu.make_async_copy(b, d, out_sem.at[i]) for i, (_, b, d) in enumerate(pairs)]
    for c in first:
        c.start()
    for c, d in zip(first, second):
        c.wait()
        d.start()
    for d in second:
        d.wait()


def padded(*lead):
    return pltpu.VMEM((*lead, ROWS, TY), F32)


def on_device(adjoint_prev, viscosity, friction, basal_velocity, ice_mask, misfit, block_tile, block_row):
    hbm = pl.BlockSpec(memory_space=pltpu.HBM)
    dma = pltpu.SemaphoreType.DMA
    shapes = (jax.ShapeDtypeStruct((2, LAYERS, TX, TY), F32), jax.ShapeDtypeStruct((TX, TY), F32))
    results = pl.pallas_call(
        kernel,
        out_shape=shapes,
        in_specs=[hbm] * 8,
        out_specs=(hbm, hbm),
        scratch_shapes=[
            padded(2, LAYERS + 2), padded(2, LAYERS + 2), padded(LAYERS + 2),
            padded(LAYERS), padded(LAYERS), padded(LAYERS), padded(LAYERS),
            pltpu.VMEM((TX, TY), jnp.int32), padded(), padded(),
            pltpu.VMEM((4, 80, 128), F32), pltpu.VMEM((4, 80, 128), F32), pltpu.VMEM((4, 80, 128), F32),
            pltpu.VMEM((2, 62, 4, 128), F32), pltpu.VMEM((2, 62, 4, 128), F32),
            padded(2, 3), padded(2, 3), padded(2, 3), padded(3), padded(3), padded(), padded(2, 3),
            padded(4, 3), padded(2, 3), padded(2, 3),
            padded(2, 2), padded(2, 2), padded(2, 2), padded(2),
            padded(2), padded(2), padded(2), padded(2),
            pltpu.VMEM((2, TX, TY), F32), pltpu.VMEM((TX, TY), F32),
            pltpu.VMEM((1, SB), jnp.int32), pltpu.VMEM((1, SB), jnp.int32), pltpu.VMEM((1, SB), F32),
            pltpu.VMEM((2 * SB, TY), BF16), pltpu.VMEM((2 * SB, TY), F32), pltpu.VMEM((SB, 2 * TY), BF16),
            pltpu.VMEM((TILES, CAP, 2 * TY), BF16), pltpu.VMEM((TILES, CAP, 2 * TY), BF16),
            pltpu.VMEM((TILES, 1, 128), F32), pltpu.VMEM((TILES, 1, 128), F32),
            pltpu.VMEM((TX, 2 * TY), F32),
            padded(2), padded(2, 2), pltpu.VMEM((2, 3, TX, TY), F32),
            padded(3), padded(2), padded(2, 2), padded(2), padded(2),
            padded(4), padded(2, 2), padded(3, 2), padded(3, 2),
            dma((8,)), dma, dma((GX,)), dma, dma((GX,)),
            dma((8,)), dma((8,)), dma((2,)), dma((2,)), dma((10,)), dma((10,)), dma((3,)),
            pltpu.SemaphoreType.REGULAR,
        ],
        compiler_params=pltpu.CompilerParams(
            collective_id=0, has_side_effects=True, vmem_limit_bytes=60 * 2**20
        ),
    )(
        adjoint_prev, viscosity, friction, basal_velocity, ice_mask,
        misfit.reshape(2 * SB, TY), block_tile.reshape(1, SB), block_row.reshape(1, SB),
    )
    return pl.pallas_call(
        hand_on,
        out_shape=shapes,
        in_specs=[hbm] * 2,
        out_specs=(hbm, hbm),
        scratch_shapes=[pltpu.VMEM((2, LAYERS, TX, TY), F32), pltpu.VMEM((TX, TY), F32), dma((9,)), dma((9,))],
        compiler_params=pltpu.CompilerParams(vmem_limit_bytes=60 * 2**20),
    )(*results)


def solution(mesh):
    placed = (
        P(None, None, "gx", "gy"),
        P(None, "gx", "gy"),
        P("gx", "gy"),
        P(None, "gx", "gy"),
        P("gx", "gy"),
        P(("gx", "gy"), None, None),
        P(("gx", "gy"), None),
        P(("gx", "gy")),
    )
    return jax.shard_map(
        on_device,
        mesh=mesh,
        in_specs=placed,
        out_specs=(P(None, None, "gx", "gy"), P("gx", "gy")),
        check_vma=False,
    )
```

```python
import functools
import math

import jax
import jax.numpy as jnp
from jax import lax
from jax.experimental import pallas as pl
from jax.experimental.pallas import tpu as pltpu
from jax.sharding import PartitionSpec as P

ITERS = 3
GX = 8
GY = 16
TILES = GX * GY
CAP = 16
SB = 1024
LAYERS = 20
TX = 64
TY = 128
BASE = 16
ROWS = 96
F32 = jnp.float32
BF16 = jnp.bfloat16
MESH = pl.DeviceIdType.MESH
SIDES = ((0, -1), (0, 1), (-1, 0), (1, 0), (-1, -1), (-1, 1), (1, -1), (1, 1))


def omega_list(count):
    return [1.0 / (1.3 + 1.2 * math.cos((2 * k + 1) * math.pi / (2 * count))) for k in range(count)]


def lanes():
    return lax.broadcasted_iota(jnp.int32, (8, 128), 1)


def roll(x, shift):
    return pltpu.roll(x, shift, 1)


def two_n(e, f, o, heavy_x):
    exm, exp_, eym, eyp = e
    fxm, fxp, fym, fyp = f
    dym, dyp, dxm, dxp = o
    if heavy_x:
        fxm, fxp = 4.0 * fxm, 4.0 * fxp
        total = exm * (fxm - dym) + exp_ * (fxp + dyp) + (eym * (fym - 0.5 * dxm) + eyp * (fyp + 0.5 * dxp))
    else:
        fym, fyp = 4.0 * fym, 4.0 * fyp
        total = exm * (fxm - 0.5 * dym) + exp_ * (fxp + 0.5 * dyp) + (eym * (fym - dxm) + eyp * (fyp + dxp))
    return total, (fxm + fxp) + (fym + fyp)


def kernel(
    adj_hbm, eta_hbm, fric_hbm, vel_hbm, ice_hbm, mis_hbm, tile_hbm, row_hbm,
    out_hbm, grad_hbm,
    fa, fb, et, eym, eyp, gu, gv, icei, icef, frip,
    e_own, e_left, e_right, pr, rr, s0, s1, s2, se, si, sf, sg, sn, sym, syp, h0, h1, h2, he, yma, ypa, ymb, ypb,
    vel_v, grad_v, tile_v, row_v, slot_v, mis_v, mis_f, vals, sendb, recvb, rsend, rrecv, surf,
    c1, c2, c3, ec, tc1, tc2, tym, typ, te, tg, ycm, ycp,
    in_sem, a_send, a_recv, r_send, r_recv, h_send, h_recv, q_send, q_recv, c_send, c_recv, o_sem, bar2,
):
    me_x = lax.axis_index("gx")
    me_y = lax.axis_index("gy")
    me = me_x * GY + me_y
    omegas = omega_list(ITERS)

    def at(dx, dy):
        return (lax.rem(me_x + dx + GX, GX), lax.rem(me_y + dy + GY, GY))

    def alone(step):
        lax.fori_loop(0, jnp.minimum(me_x, 0) + 1, lambda i, carry: (step(), carry)[1], 0)

    ins = [
        (tile_hbm, tile_v), (row_hbm, row_v), (mis_hbm, mis_v),
        (vel_hbm, vel_v), (ice_hbm, icei), (fric_hbm, frip.at[pl.ds(BASE, TX)]),
        (eta_hbm, et.at[pl.ds(1, LAYERS), pl.ds(BASE, TX)]),
        (adj_hbm, fa.at[:, pl.ds(1, LAYERS), pl.ds(BASE, TX)]),
    ]
    loads = [pltpu.make_async_copy(s, d, in_sem.at[i]) for i, (s, d) in enumerate(ins)]
    for c in loads:
        c.start()
    barrier = pltpu.get_barrier_semaphore()
    for k in range(1, GY):
        pl.semaphore_signal(barrier, inc=1, device_id=at(0, k), device_id_type=MESH)
    for k in range(1, GX):
        pl.semaphore_signal(barrier, inc=1, device_id=at(k, 0), device_id_type=MESH)
    for dx, dy in SIDES[4:]:
        pl.semaphore_signal(barrier, inc=1, device_id=at(dx, dy), device_id_type=MESH)


    for c in loads[4:]:
        c.wait()
    lane = lanes()

    def build(rb, carry):
        r = pl.multiple_of(BASE + rb * 8, 8)
        q = pl.multiple_of(8 + rb * 8, 8)
        ice = icei[pl.ds(pl.multiple_of(rb * 8, 8), 8)].astype(F32)
        icef[pl.ds(r, 8)] = ice
        edge = jnp.zeros((8, 128), F32)

        def put(acc, x, unit):
            return jnp.where((lane >= 8 * unit) & (lane < 8 * unit + 8), roll(x, (8 * unit + 4) % 128), acc)

        for kind in range(3):
            acc = jnp.zeros((8, 128), F32)
            for l in range(LAYERS):
                if kind < 2:
                    x = ice * fa[kind, l + 1, pl.ds(r, 8)]
                    fa[kind, l + 1, pl.ds(r, 8)] = x
                else:
                    x = et[l + 1, pl.ds(r, 8)]
                if l < 16:
                    acc = put(acc, x, l)
                else:
                    edge = put(edge, x, 4 * kind + l - 16)
            e_own[kind, pl.ds(q, 8)] = acc
        edge = put(edge, ice, 12)
        edge = put(edge, frip[pl.ds(r, 8)], 13)
        e_own[3, pl.ds(q, 8)] = edge
        return carry

    lax.fori_loop(0, 8, build, 0)

    def pack_rows(l, carry):
        for up in range(2):
            r = BASE + (TX - 4) * up
            pr[up, l] = fa[0, l + 1, pl.ds(r, 4)]
            pr[up, LAYERS + l] = fa[1, l + 1, pl.ds(r, 4)]
            pr[up, 2 * LAYERS + l] = et[l + 1, pl.ds(r, 4)]
        return carry

    lax.fori_loop(0, LAYERS, pack_rows, 0)
    for up in range(2):
        r = BASE + (TX - 4) * up
        pr[up, 3 * LAYERS] = icef[pl.ds(r, 4)]
        pr[up, 3 * LAYERS + 1] = frip[pl.ds(r, 4)]

    pl.semaphore_wait(barrier, GX + GY + 2)
    for k in range(1, GX):
        pl.semaphore_signal(bar2, inc=1, device_id=at(k, 0), device_id_type=MESH)

    def span(dx):
        if dx == 0:
            return pl.ds(8, TX), pl.ds(8, TX)
        return (pl.ds(8, 8), pl.ds(72, 8)) if dx < 0 else (pl.ds(64, 8), pl.ds(0, 8))

    halos = []
    for i, (dx, dy) in enumerate(SIDES):
        src, dst = span(dx)
        land = (e_right, e_own, e_left)[dy + 1]
        halos.append(
            pltpu.make_async_remote_copy(
                e_own.at[:, src], land.at[:, dst], h_send.at[i], h_recv.at[i],
                device_id=at(dx, dy), device_id_type=MESH,
            )
        )
    for up, dx in ((0, -1), (1, 1)):
        halos.append(
            pltpu.make_async_remote_copy(
                pr.at[up], rr.at[1 - up], q_send.at[up], q_recv.at[up], device_id=at(dx, 0), device_id_type=MESH
            )
        )
    for c in halos:
        c.start()

    loads[0].wait()
    loads[1].wait()
    ii = lax.broadcasted_iota(jnp.int32, (256, 512), 0)
    jj = lax.broadcasted_iota(jnp.int32, (256, 512), 1)
    tri = jnp.where((ii < jj) | (jj >= 256), 1.0, 0.0).astype(BF16)
    tsub = lax.broadcasted_iota(jnp.int32, (TILES, 256), 0)
    running = jnp.zeros((TILES, 256), F32)
    rmat = jnp.zeros((TILES, 128), F32)
    for c in range(4):
        t = tile_v[:, pl.ds(256 * c, 256)]
        hit = jnp.where(t == tsub, 1.0, 0.0)
        hot = hit.astype(BF16)
        sums = jnp.dot(hot, tri, preferred_element_type=F32)
        pos = jnp.sum(hit * (running + sums[:, :256]), axis=0, keepdims=True)
        running = running + sums[:, 256:]
        slot_v[:, pl.ds(256 * c, 256)] = t.astype(F32) * float(CAP) + pos
        z = jnp.where(
            pos == (tsub & (CAP - 1)).astype(F32), row_v[:, pl.ds(256 * c, 256)].astype(F32) + 1.0, 0.0
        ).astype(BF16)
        rmat = rmat + lax.dot_general(hot, z, (((1,), (1,)), ((), ())), preferred_element_type=F32)
    rsend[...] = rmat.reshape(TILES, 1, 128)

    loads[2].wait()

    def widen(i, carry):
        mis_f[pl.ds(pl.multiple_of(i * 128, 128), 128)] = mis_v[pl.ds(pl.multiple_of(i * 128, 128), 128)].astype(F32)
        return carry

    lax.fori_loop(0, 16, widen, 0)
    for c in range(2):
        for i in range(8):
            vals[pl.ds(128 * i, 128), pl.ds(128 * c, 128)] = mis_f[pl.ds(256 * i + c, 128, stride=2)].astype(BF16)

    def pack(px, carry):
        want = (px * (GY * CAP)).astype(F32) + lax.broadcasted_iota(jnp.int32, (256, SB), 0).astype(F32)
        sel = jnp.where(slot_v[...] == want, 1.0, 0.0).astype(BF16)
        got = jnp.dot(sel, vals[...], preferred_element_type=F32).astype(BF16)
        sendb[pl.ds(px * GY, GY)] = got.reshape(GY, CAP, 2 * TY)
        return carry

    lax.fori_loop(0, GX, pack, 0)

    pl.semaphore_wait(bar2, GX - 1)
    own_rows = pltpu.make_async_copy(rsend.at[me], rrecv.at[me], r_recv.at[0])
    own_rows.start()

    def send(j, carry):
        px = lax.rem(me_x + j, GX)

        def one(k, inner):
            py = lax.rem(me_y + k, GY)
            d = px * GY + py
            pltpu.make_async_remote_copy(
                rsend.at[d], rrecv.at[me], r_send, r_recv.at[j], device_id=(px, py), device_id_type=MESH
            ).start()
            return inner

        lax.fori_loop(jnp.where(j == 0, 1, 0), GY, one, 0)
        return carry

    lax.fori_loop(0, GX, send, 0)

    own_values = pltpu.make_async_copy(sendb.at[me], recvb.at[me], a_recv.at[0])
    own_values.start()

    def send_values(j, carry):
        px = lax.rem(me_x + j, GX)

        def one(k, inner):
            py = lax.rem(me_y + k, GY)
            d = px * GY + py
            pltpu.make_async_remote_copy(
                sendb.at[d], recvb.at[me], a_send, a_recv.at[j], device_id=(px, py), device_id_type=MESH
            ).start()
            return inner

        lax.fori_loop(jnp.where(j == 0, 1, 0), GY, one, 0)
        return carry

    lax.fori_loop(0, GX, send_values, 0)

    zero = jnp.zeros((8, 128), F32)

    def clear(r, carry):
        q = pl.ds(pl.multiple_of(r * 8, 8), 8)
        for end in (0, LAYERS + 1):
            et[end, q] = zero
            for c in range(2):
                fa[c, end, q] = zero
                fb[c, end, q] = zero
        return carry

    lax.fori_loop(0, ROWS // 8, clear, 0)

    def flag(cond):
        return jnp.where(cond, 1.0, 0.0).astype(F32)

    has_up, has_down = flag(me_x > 0), flag(me_x < GX - 1)
    has_left, has_right = flag(me_y > 0), flag(me_y < GY - 1)
    for c in halos:
        c.wait()

    def unpack_rows(l, carry):
        for side, r, has in ((0, BASE - 4, has_up), (1, BASE + TX, has_down)):
            fa[0, l + 1, pl.ds(r, 4)] = rr[side, l] * has
            fa[1, l + 1, pl.ds(r, 4)] = rr[side, LAYERS + l] * has
            et[l + 1, pl.ds(r, 4)] = rr[side, 2 * LAYERS + l] * has
        return carry

    lax.fori_loop(0, LAYERS, unpack_rows, 0)
    for side, r, has in ((0, BASE - 4, has_up), (1, BASE + TX, has_down)):
        icef[pl.ds(r, 4)] = rr[side, 3 * LAYERS] * has
        frip[pl.ds(r, 4)] = rr[side, 3 * LAYERS + 1] * has

    low4 = (lane & 7) < 4

    def tile_units(x):
        x = jnp.where(lane < 8, x, 0.0)
        for s in (8, 16, 32, 64):
            x = x + roll(x, s)
        return x

    right = lane < 64
    half = (lane & 63) < 32

    def join(a, b):
        return jnp.where(right, a, roll(b, 64))

    def halo(dst, x, w):
        dst[0, w] = jnp.where(low4, x[1], x[0])
        dst[1, w] = jnp.where(low4, roll(x[2], 64), x[2])

    for b in range(10):
        q = pl.ds(8 * b, 8)
        w = pl.ds(8 + 8 * b, 8)
        has = has_up if b == 0 else (has_down if b == 9 else 1.0)
        r_, l_ = [], []
        for kind in range(4):
            own = e_own[kind, q] * has
            r_.append(jnp.where(low4, own, e_right[kind, q] * (has * has_right)))
            l_.append(jnp.where(low4, e_left[kind, q] * (has * has_left), own))
        for c in range(3):
            turn = (0, 96, 64)[c]
            mr, ml = (roll(r_[3], turn), roll(l_[3], turn)) if turn else (r_[3], l_[3])
            x = (r_[c], l_[c], jnp.where(half, join(mr, ml), 0.0))
            for p in range(3):
                if c < 2:
                    s0[c, p, w] = x[p]
                else:
                    se[p, w] = x[p]
            halo((h0.at[0], h0.at[1], he)[c], x, w)
        a, d = tile_units(roll(r_[3], 32)), tile_units(roll(l_[3], 32))
        si[0, w] = a
        si[1, w] = d
        si[2, w] = jnp.where(half, jnp.where(right, a, d), 0.0)
        sf[w] = jnp.where(half & ((lane & 63) >= 24), join(roll(r_[3], 48), roll(l_[3], 48)), 0.0)

    def inverse(dx4, dy4, rest, ice):
        du = 4.0 * dx4 + dy4 + rest
        dv = dx4 + 4.0 * dy4 + rest
        live = ice > 0.0
        r = jnp.where(live, 0.5, 0.0) / jnp.where(live, du * dv, 1.0)
        return r * dv, r * du

    def neighbours(x, p):
        if p < 2:
            return (
                jnp.where(lane < 8, 0.0, roll(x[p], 8)),
                jnp.where(lane < 120, roll(x[p], 120), roll(x[2], 120 if p == 0 else 56)),
            )
        up = jnp.where(right, jnp.where(lane < 8, roll(x[0], 8), roll(x[2], 8)), 0.0)
        return (
            jnp.where(right, up, jnp.where(lane < 72, roll(x[1], 72), roll(x[2], 8))),
            roll(x[2], 120),
        )

    starts = [14 + 8 * b for b in range(9)]

    for r in starts:
        w = pl.ds(r, 8)
        es = [se[p, w] for p in range(3)]
        for p, e in enumerate(es):
            up, down = neighbours(es, p)
            count = jnp.where((lane < 8) if p < 2 else ((lane & 63) >= 24), 1.0, 2.0)
            dx4 = 0.5 * (se[p, pl.ds(r - 1, 8)] + se[p, pl.ds(r + 1, 8)]) + e
            ym, yp = roll(e, 1), roll(e, 127)
            for k, x in enumerate((ym, yp, up, down)):
                sn[k, p, w] = x
            dy4 = 0.5 * (ym + yp) + e
            rest = 2.0 * (up + down + count * e)
            if p == 2:
                rest = rest + sf[w]
            a, b = inverse(dx4, dy4, rest, si[p, w])
            sg[0, p, w] = a
            sg[1, p, w] = b

    def shifted(x, beyond):
        return roll(jnp.where(lane == 127, beyond, x), 1), roll(jnp.where(lane == 0, beyond, x), 127)

    def main_inverse(l):
        g = l // 16
        unit = l - 16 * g
        turn = 124 - 8 * unit
        bottom = flag(l == LAYERS - 1)
        count = 2.0 - flag(l == 0) - bottom
        for r in starts:
            w = pl.ds(r, 8)
            e = et[l + 1, w]
            ym, yp = shifted(e, roll(he[g, w], turn))
            eym[l, w] = ym
            eyp[l, w] = yp
            dx4 = 0.5 * (et[l + 1, pl.ds(r - 1, 8)] + et[l + 1, pl.ds(r + 1, 8)]) + e
            dy4 = 0.5 * (ym + yp) + e
            rest = 2.0 * (et[l, w] + et[l + 2, w] + count * e) + bottom * frip[w]
            a, b = inverse(dx4, dy4, rest, icef[w])
            gu[l, w] = a
            gv[l, w] = b

    def inverses(i, carry):
        for k in range(4):
            main_inverse(4 * i + k)
        return carry

    lax.fori_loop(0, LAYERS // 4, inverses, 0)

    def strip_sweep(src, dst, beyond, omega):
        for b in range(1, 11):
            w = pl.ds(8 * b, 8)
            for c in range(2):
                for p in range(3):
                    x = src[c, p, w]
                    sym[c, p, w] = roll(x, 1)
                    syp[c, p, w] = roll(x, 127)
        for r in starts:
            w, wm, wp = pl.ds(r, 8), pl.ds(r - 1, 8), pl.ds(r + 1, 8)
            mid = [[src[c, p, w] for p in range(3)] for c in range(2)]
            new = [[None] * 3 for _ in range(2)]
            for p in range(3):
                e, eu, ed = se[p, w], sn[2, p, w], sn[3, p, w]
                faces = (se[p, wm], se[p, wp], sn[0, p, w], sn[1, p, w])
                own, diffs = [], []
                for c in range(2):
                    own.append((src[c, p, wm], src[c, p, wp], sym[c, p, w], syp[c, p, w]))
                    mm, mp, pm, pp = sym[c, p, wm], syp[c, p, wm], sym[c, p, wp], syp[c, p, wp]
                    diffs.append((mp - mm, pp - pm, pm - mm, pp - mp))
                for c in range(2):
                    up, down = neighbours(mid[c], p)
                    total, near = two_n(faces, own[c], diffs[1 - c], c == 0)
                    total = total + e * (near + 4.0 * (up + down)) + 4.0 * (eu * up + ed * down)
                    new[c][p] = (1.0 - omega) * mid[c][p] + omega * (sg[c, p, w] * total)
                    dst[c, p, w] = new[c][p]
            for c in range(2):
                halo(beyond.at[c], new[c], w)

    def main_sweep(src, beyond, omega, first, rows_at, store):
        def shift(l, ym_, yp_):
            g = l // 16
            turn = 124 - 8 * (l - 16 * g)
            for b in range(9):
                w = pl.ds(first + 8 * b, 8)
                for c in range(2):
                    ym, yp = shifted(src[c, l + 1, w], roll(beyond[c, g, w], turn))
                    ym_[c, w] = ym
                    yp_[c, w] = yp

        def sweep(l, ym_, yp_):
            for r in rows_at:
                w, wm, wp = pl.ds(r, 8), pl.ds(r - 1, 8), pl.ds(r + 1, 8)
                e, eu, ed = et[l + 1, w], et[l, w], et[l + 2, w]
                faces = (et[l + 1, wm], et[l + 1, wp], eym[l, w], eyp[l, w])
                own, diffs = [], []
                for c in range(2):
                    own.append((src[c, l + 1, wm], src[c, l + 1, wp], ym_[c, w], yp_[c, w]))
                    mm, mp, pm, pp = ym_[c, wm], yp_[c, wm], ym_[c, wp], yp_[c, wp]
                    diffs.append((mp - mm, pp - pm, pm - mm, pp - mp))
                for c in range(2):
                    up, down = src[c, l, w], src[c, l + 2, w]
                    total, near = two_n(faces, own[c], diffs[1 - c], c == 0)
                    total = total + e * (near + 4.0 * (up + down)) + 4.0 * (eu * up + ed * down)
                    inv = (gu, gv)[c][l, w]
                    store(c, l, r, (1.0 - omega) * src[c, l + 1, w] + omega * (inv * total))

        def pair(i, carry):
            l = 2 * i
            shift(l + 1, ymb, ypb)
            sweep(l, yma, ypa)
            shift(l + 2, yma, ypa)
            sweep(l + 1, ymb, ypb)
            return carry

        shift(0, yma, ypa)
        lax.fori_loop(0, LAYERS // 2, pair, 0)

    def store_to(dst):
        def store(c, l, r, x):
            dst[c, l + 1, pl.ds(r, 8)] = x

        return store

    main_sweep(fa, h0, omegas[0], 13, starts, store_to(fb))
    strip_sweep(s0, s1, h1, omegas[0])
    main_sweep(fb, h1, omegas[1], 14, [15 + 8 * b for b in range(9)], store_to(fa))

    group = lane // CAP
    sub8 = lax.broadcasted_iota(jnp.int32, (8, 128), 0)
    sub64 = lax.broadcasted_iota(jnp.int32, (TX, 256), 0).astype(F32) + 1.0
    for j in range(GX):
        here = pl.ds(lax.rem(me_x - j + GX, GX) * GY, GY)
        pltpu.make_async_copy(recvb.at[here], recvb.at[here], a_recv.at[j]).wait()
        pltpu.make_async_copy(rrecv.at[here], rrecv.at[here], r_recv.at[j]).wait()
    total = jnp.zeros((TX, 2 * TY), F32)
    for j in range(GX):
        rows = rrecv[pl.ds(j * GY, GY)].reshape(GY, 128)
        parts = [
            jnp.sum(jnp.where(sub8 == group, rows[8 * h : 8 * h + 8], 0.0), axis=0, keepdims=True) for h in range(2)
        ]
        hot = jnp.where(jnp.concatenate(parts, axis=1) == sub64, 1.0, 0.0).astype(BF16)
        got = recvb[pl.ds(j * GY, GY)].reshape(GY * CAP, 2 * TY)
        total = total + jnp.dot(hot, got, preferred_element_type=F32)
    surf[...] = total

    for b in range(8):
        w = pl.ds(BASE + 8 * b, 8)
        cu = (2.0 * omegas[0]) * (gu[0, w] * surf[pl.ds(8 * b, 8), pl.ds(0, 128)])
        cv = (2.0 * omegas[0]) * (gv[0, w] * surf[pl.ds(8 * b, 8), pl.ds(128, 128)])
        c1[0, w] = cu
        c1[1, w] = cv
        ec[1, w] = jnp.where(lane < 8, roll(cu, 4), roll(cv, 12))

    def span_c(dx):
        if dx == 0:
            return pl.ds(BASE, TX), pl.ds(BASE, TX)
        if dx < 0:
            return pl.ds(BASE, 8), pl.ds(BASE + TX, 8)
        return pl.ds(BASE + TX - 8, 8), pl.ds(BASE - 8, 8)

    edges = []
    for i, (dx, dy) in enumerate(SIDES):
        src, dst = span_c(dx)
        edges.append(
            pltpu.make_async_remote_copy(
                ec.at[1, src], ec.at[1 - dy, dst], c_send.at[i], c_recv.at[i],
                device_id=at(dx, dy), device_id_type=MESH,
            )
        )
    for up, dx in ((0, -1), (1, 1)):
        src, dst = span_c(dx)
        edges.append(
            pltpu.make_async_remote_copy(
                c1.at[:, src], c1.at[:, dst], c_send.at[8 + up], c_recv.at[8 + up],
                device_id=at(dx, 0), device_id_type=MESH,
            )
        )
    for c in edges:
        c.start()

    strip_sweep(s1, s2, h2, omegas[1])
    main_sweep(fa, h2, omegas[2], 15, [BASE + 8 * b for b in range(8)], store_to(fb))
    kept = pl.ds(4, LAYERS - 3)
    out_low = pltpu.make_async_copy(fb.at[:, kept, pl.ds(BASE, TX)], out_hbm.at[:, pl.ds(3, LAYERS - 3)], o_sem.at[0])
    out_low.start()
    loads[3].wait()
    for b in range(8):
        r, w = pl.ds(8 * b, 8), pl.ds(BASE + 8 * b, 8)
        flow = vel_v[0, r] * fb[0, LAYERS, w] + vel_v[1, r] * fb[1, LAYERS, w]
        grad_v[r] = -frip[w] * icef[w] * flow
    out_grad = pltpu.make_async_copy(grad_v, grad_hbm, o_sem.at[2])
    out_grad.start()
    for r in starts:
        w = pl.ds(r, 8)
        te[1, w] = join(roll(se[0, w], 120), roll(se[1, w], 120))
        for c in range(2):
            a, b = sg[c, 0, w], sg[c, 1, w]
            tg[0, c, w] = join(a, b)
            tg[1, c, w] = join(roll(a, 120), roll(b, 120))
    for b in range(1, 11):
        w = pl.ds(8 * b, 8)
        e = join(se[0, w], se[1, w])
        te[0, w] = e
        te[2, w] = roll(e, 1)
        te[3, w] = roll(e, 127)

    for c in edges:
        c.wait()

    for w, has in ((pl.ds(BASE - 8, 8), has_up), (pl.ds(BASE + TX, 8), has_down)):
        for c in range(2):
            c1[c, w] = c1[c, w] * has
    for b in range(1, 11):
        w = pl.ds(8 * b, 8)
        has = has_up if b == 1 else (has_down if b == 10 else 1.0)
        own, lef, rig = ec[1, w] * has, ec[0, w] * (has * has_left), ec[2, w] * (has * has_right)
        r_, l_, out = jnp.where(low4, own, rig), jnp.where(low4, lef, own), jnp.where(low4, lef, rig)
        for c in range(2):
            ym, yp = shifted(c1[c, w], roll(out, 124 - 8 * c))
            ycm[0, c, w] = ym
            ycp[0, c, w] = yp
            t = jnp.where(right, roll(r_, 120), roll(l_, 56)) if c else join(r_, l_)
            tc1[c, w] = t
            tym[c, w] = roll(t, 1)
            typ[c, w] = roll(t, 127)

    w1, w2 = omegas[1], omegas[2]
    again1 = 1.0 - w1 + w1 / omegas[0]
    def edge_strips():
        for r in starts:
            w, wm, wp = pl.ds(r, 8), pl.ds(r - 1, 8), pl.ds(r + 1, 8)
            e = te[0, w]
            faces = (te[0, wm], te[0, wp], te[2, w], te[3, w])
            own, diffs, mid = [], [], []
            for c in range(2):
                mid.append(tc1[c, w])
                own.append((tc1[c, wm], tc1[c, wp], tym[c, w], typ[c, w]))
                mm, mp, pm, pp = tym[c, wm], typ[c, wm], tym[c, wp], typ[c, wp]
                diffs.append((mp - mm, pp - pm, pm - mm, pp - mp))
            for c in range(2):
                total, near = two_n(faces, own[c], diffs[1 - c], c == 0)
                for l, t in enumerate((
                    again1 * mid[c] + w1 * (tg[0, c, w] * (total + e * near)),
                    (4.0 * w1) * (tg[1, c, w] * ((e + te[1, w]) * mid[c])),
                )):
                    tc2[l, c, w] = jnp.where(right, roll(t, 124), roll(t, 60))

    alone(edge_strips)

    def around(src, slot, l, w, wm, wp):
        e = et[l + 1, w]
        faces = (et[l + 1, wm], et[l + 1, wp], eym[l, w], eyp[l, w])
        own, diffs = [], []
        for c in range(2):
            own.append((src(c, wm), src(c, wp), ycm[slot, c, w], ycp[slot, c, w]))
            mm, mp, pm, pp = ycm[slot, c, wm], ycp[slot, c, wm], ycm[slot, c, wp], ycp[slot, c, wp]
            diffs.append((mp - mm, pp - pm, pm - mm, pp - mp))
        sums = []
        for c in range(2):
            total, near = two_n(faces, own[c], diffs[1 - c], c == 0)
            sums.append(total + e * near)
        return sums

    def second():
        for r in starts:
            w, wm, wp = pl.ds(r, 8), pl.ds(r - 1, 8), pl.ds(r + 1, 8)
            sums = around(lambda c, x: c1[c, x], 0, 0, w, wm, wp)
            pair = et[1, w] + et[2, w]
            for c in range(2):
                z = c1[c, w]
                for l, x in enumerate((
                    again1 * z + w1 * ((gu, gv)[c][0, w] * sums[c]),
                    (4.0 * w1) * ((gu, gv)[c][1, w] * (pair * z)),
                )):
                    c2[l, c, w] = x
                    ym, yp = shifted(x, tc2[l, c, w])
                    ycm[1 + l, c, w] = ym
                    ycp[1 + l, c, w] = yp

    alone(second)

    def third():
        for b in range(8):
            r = BASE + 8 * b
            w, wm, wp = pl.ds(r, 8), pl.ds(r - 1, 8), pl.ds(r + 1, 8)
            pair = 4.0 * (et[1, w] + et[2, w])
            next_pair = (4.0 * w2) * (et[2, w] + et[3, w])
            for l in range(2):
                sums = around(lambda c, x: c2[l, c, x], 1 + l, l, w, wm, wp)
                for c in range(2):
                    total = sums[c] + pair * c2[1 - l, c, w]
                    x = (1.0 - w2) * c2[l, c, w] + w2 * ((gu, gv)[c][l, w] * total)
                    if l == 0:
                        x = x + (w2 / omegas[0]) * c1[c, w]
                    c3[c, l, pl.ds(8 * b, 8)] = fb[c, l + 1, w] + x
            for c in range(2):
                x = (gu, gv)[c][2, w] * (next_pair * c2[1, c, w])
                c3[c, 2, pl.ds(8 * b, 8)] = fb[c, 3, w] + x

    alone(third)

    out_high = pltpu.make_async_copy(c3, out_hbm.at[:, pl.ds(0, 3)], o_sem.at[1])
    out_high.start()

    pltpu.make_async_copy(sendb.at[pl.ds(0, TILES - 1)], sendb.at[pl.ds(0, TILES - 1)], a_send).wait()
    pltpu.make_async_copy(rsend.at[pl.ds(0, TILES - 1)], rsend.at[pl.ds(0, TILES - 1)], r_send).wait()
    out_low.wait()
    out_high.wait()
    out_grad.wait()


def hand_on(adj_ref, grad_ref, out_ref, grad_out_ref, held, grad_held, in_sem, out_sem):
    pairs = []
    for c in range(2):
        for k in range(4):
            at = (c, pl.ds(k * (LAYERS // 4), LAYERS // 4))
            pairs.append((adj_ref.at[at], held.at[at], out_ref.at[at]))
    pairs.append((grad_ref, grad_held, grad_out_ref))
    first = [pltpu.make_async_copy(a, b, in_sem.at[i]) for i, (a, b, _) in enumerate(pairs)]
    second = [pltpu.make_async_copy(b, d, out_sem.at[i]) for i, (_, b, d) in enumerate(pairs)]
    for c in first:
        c.start()
    for c, d in zip(first, second):
        c.wait()
        d.start()
    for d in second:
        d.wait()


def padded(*lead):
    return pltpu.VMEM((*lead, ROWS, TY), F32)


def on_device(adjoint_prev, viscosity, friction, basal_velocity, ice_mask, misfit, block_tile, block_row):
    hbm = pl.BlockSpec(memory_space=pltpu.HBM)
    dma = pltpu.SemaphoreType.DMA
    shapes = (jax.ShapeDtypeStruct((2, LAYERS, TX, TY), F32), jax.ShapeDtypeStruct((TX, TY), F32))
    results = pl.pallas_call(
        kernel,
        out_shape=shapes,
        in_specs=[hbm] * 8,
        out_specs=(hbm, hbm),
        scratch_shapes=[
            padded(2, LAYERS + 2), padded(2, LAYERS + 2), padded(LAYERS + 2),
            padded(LAYERS), padded(LAYERS), padded(LAYERS), padded(LAYERS),
            pltpu.VMEM((TX, TY), jnp.int32), padded(), padded(),
            pltpu.VMEM((4, 80, 128), F32), pltpu.VMEM((4, 80, 128), F32), pltpu.VMEM((4, 80, 128), F32),
            pltpu.VMEM((2, 62, 4, 128), F32), pltpu.VMEM((2, 62, 4, 128), F32),
            padded(2, 3), padded(2, 3), padded(2, 3), padded(3), padded(3), padded(), padded(2, 3),
            padded(4, 3), padded(2, 3), padded(2, 3),
            padded(2, 2), padded(2, 2), padded(2, 2), padded(2),
            padded(2), padded(2), padded(2), padded(2),
            pltpu.VMEM((2, TX, TY), F32), pltpu.VMEM((TX, TY), F32),
            pltpu.VMEM((1, SB), jnp.int32), pltpu.VMEM((1, SB), jnp.int32), pltpu.VMEM((1, SB), F32),
            pltpu.VMEM((2 * SB, TY), BF16), pltpu.VMEM((2 * SB, TY), F32), pltpu.VMEM((SB, 2 * TY), BF16),
            pltpu.VMEM((TILES, CAP, 2 * TY), BF16), pltpu.VMEM((TILES, CAP, 2 * TY), BF16),
            pltpu.VMEM((TILES, 1, 128), F32), pltpu.VMEM((TILES, 1, 128), F32),
            pltpu.VMEM((TX, 2 * TY), F32),
            padded(2), padded(2, 2), pltpu.VMEM((2, 3, TX, TY), F32),
            padded(3), padded(2), padded(2, 2), padded(2), padded(2),
            padded(4), padded(2, 2), padded(3, 2), padded(3, 2),
            dma((8,)), dma, dma((GX,)), dma, dma((GX,)),
            dma((8,)), dma((8,)), dma((2,)), dma((2,)), dma((10,)), dma((10,)), dma((3,)),
            pltpu.SemaphoreType.REGULAR,
        ],
        compiler_params=pltpu.CompilerParams(
            collective_id=0, has_side_effects=True, vmem_limit_bytes=60 * 2**20
        ),
    )(
        adjoint_prev, viscosity, friction, basal_velocity, ice_mask,
        misfit.reshape(2 * SB, TY), block_tile.reshape(1, SB), block_row.reshape(1, SB),
    )
    return pl.pallas_call(
        hand_on,
        out_shape=shapes,
        in_specs=[hbm] * 2,
        out_specs=(hbm, hbm),
        scratch_shapes=[pltpu.VMEM((2, LAYERS, TX, TY), F32), pltpu.VMEM((TX, TY), F32), dma((9,)), dma((9,))],
        compiler_params=pltpu.CompilerParams(vmem_limit_bytes=60 * 2**20),
    )(*results)


def solution(mesh):
    placed = (
        P(None, None, "gx", "gy"),
        P(None, "gx", "gy"),
        P("gx", "gy"),
        P(None, "gx", "gy"),
        P("gx", "gy"),
        P(("gx", "gy"), None, None),
        P(("gx", "gy"), None),
        P(("gx", "gy")),
    )
    return jax.shard_map(
        on_device,
        mesh=mesh,
        in_specs=placed,
        out_specs=(P(None, None, "gx", "gy"), P("gx", "gy")),
        check_vma=False,
    )
```
